256 devices in a mesh: ep: 32 (over x, z), tp: 8 (over y, core).
Axes of the slice: x: 4, y: 4, z: 8, core: 2. Of those that a mesh axis runs over, the one named last changes fastest.
Arguments:
- tokens: bfloat16 [4096, 6144], P('ep', 'tp'), may hold values from -6 to 6
- cotangent: bfloat16 [4096, 6144], P('ep', 'tp'), may hold values from -6 to 6
- routes: int32 [4096, 2], P('ep'), may hold values from 0 to 7, all different within a row; in each aligned block of 128 rows (0 to 127, 128 to 255, ...) at most 40 rows name the same one
- route_gates: bfloat16 [4096, 2], P('ep'), may hold values from 0.19921875 to 1
- example_ids: int32 [32, 128], P('ep'), may hold values from 0 to 3, never falling along the last dimension, each value on 1 to 64 neighbouring positions
- gate_weight: bfloat16 [32, 6144, 2048], P('ep', None, 'tp'), may hold values from -2 to 2
- up_weight: bfloat16 [32, 6144, 2048], P('ep', None, 'tp'), may hold values from -2 to 2
Outputs:
- clipped_sum: bfloat16 [32, 2048, 6144], P('ep', None, 'tp')
- norm_ratio: float32 [128], replicated
The draws below stay inside these ranges and needn't reach their ends.
Inputs may be any that keep to these rules, and one draw needn't show every extreme that they name: `routes`: within the rows of one device (aligned blocks of 128 tokens) no expert is named more than 40 times; the 2 experts of a token differ. example_ids never falls along a row, and each of the 4 examples of a row has 1 to 64 tokens.
All inputs are finite; a program needn't handle non-finite values.
Results may differ from the reference program's by a relative error of at most 0.0012.
The reference program's roundings to bfloat16 on the way (of `hidden` and `scaled`) count: a program that leaves them out, or rounds other values in their place, can miss the bound.
Values may be sent and summed in bfloat16 or wider, within the bound.
A program may use at most 128 MiB of HBM per device.

```python
import math
import jax
import jax.numpy as jnp
import numpy as np
from jax import lax

D = 6144
FF = 8192
EXPERTS = 8
TOPK = 2
TOK_DEV = 128
EX_DEV = 4
EX_MOST = 64
CAP = 40
GROUP = 4
TOKENS = 4096
EXAMPLES = 128
N_EP = 32


def row_scales(rise):
    count = EXPERTS * GROUP
    position = jnp.arange(count, dtype=jnp.float32) / max(count - 1, 1)
    return rise ** position


def column_scales(rise, rms):
    position = jnp.arange(D, dtype=jnp.float32) / max(D - 1, 1)
    return rise ** position / rms


def draw_gate_weight(key, part):
    key = jax.random.fold_in(key, 11)
    shape = (EXPERTS * GROUP, D, FF // GROUP)
    values = jnp.clip(jax.random.normal(key, shape, jnp.float32), -6.0, 6.0) * row_scales(1.32)[:, None, None]
    return (values * D ** (-0.5)).astype(jnp.bfloat16)


def draw_up_weight(key, part):
    key = jax.random.fold_in(key, 23)
    shape = (EXPERTS * GROUP, D, FF // GROUP)
    values = jnp.clip(jax.random.normal(key, shape, jnp.float32), -6.0, 6.0) * row_scales(1.32)[:, None, None]
    return (values * D ** (-0.5)).astype(jnp.bfloat16)


def draw_tokens(key, part):
    key = jax.random.fold_in(key, 31)
    noise_key, common_key = jax.random.split(key)
    shape = (N_EP, TOK_DEV, D)
    noise = jnp.clip(jax.random.normal(noise_key, shape, jnp.float32), -5.0, 5.0)
    common = jnp.clip(jax.random.normal(common_key, (N_EP, 1, D), jnp.float32), -3.0, 3.0)
    values = 0.8 * noise + 0.6 * common
    return values.reshape(N_EP * TOK_DEV, D).astype(jnp.bfloat16)


def draw_cotangent(key, part):
    key = jax.random.fold_in(key, 37)
    noise_key, common_key = jax.random.split(key)
    shape = (N_EP, TOK_DEV, D)
    noise = jnp.clip(jax.random.normal(noise_key, shape, jnp.float32), -5.0, 5.0)
    common = jnp.clip(jax.random.normal(common_key, (N_EP, 1, D), jnp.float32), -3.0, 3.0)
    values = (0.8 * noise + 0.6 * common) * column_scales(4.0, 2.326)[None, None, :]
    values = jnp.clip(values, -6.0, 6.0)
    return values.reshape(N_EP * TOK_DEV, D).astype(jnp.bfloat16)


def block_levels(own_key, extent, pieces, least, largest):
    level = 1.0
    for dim, parts in pieces:
        draws = jax.random.uniform(jax.random.fold_in(jax.random.fold_in(own_key, 6), dim), (parts,), jnp.float32, least / len(pieces), largest / len(pieces))
        level = level * jnp.repeat(jnp.exp(draws), extent[dim] // parts).reshape((-1,) + (1,) * (len(extent) - 1 - dim))
    return level


def profile(count, total, reach, skew):
    loads = [(1 << 20) // math.isqrt(rank ** skew) + 1 for rank in range(2, count + 1)]
    surplus, holding = total - reach - (count - 1), [1] * (count - 1)
    while surplus > 0:
        movable = [i for i in range(count - 1) if holding[i] < reach]
        whole, budget = sum([loads[i] for i in movable]), surplus
        for i in movable:
            more = min(reach - holding[i], max(1, budget * loads[i] // whole), surplus)
            holding[i] = holding[i] + more
            surplus = surplus - more
    return np.array([reach] + holding)


def ragged(key, number_of, total, reach, skew):
    if number_of == 2:
        one = jax.random.randint(key, (), max(1, total - reach), min(reach, total - 1) + 1)
        return jnp.stack([one, total - one])
    lengths = jnp.asarray(profile(number_of, total, reach, skew), jnp.int32)
    pairs = (number_of - 1) // 2
    source_of, sink = lengths[1:1 + 2 * pairs:2], lengths[2:2 + 2 * pairs:2]
    room = jnp.minimum(source_of - 1, reach - sink)
    moved = jax.random.randint(jax.random.fold_in(key, 1), (pairs,), 0, 1 << 20) % (room + 1)
    lengths = lengths.at[1:1 + 2 * pairs:2].set(source_of - moved).at[2:2 + 2 * pairs:2].set(sink + moved)
    return lengths[jax.random.permutation(jax.random.fold_in(key, 2), number_of)]


def routed_block(rng, own, number, rows, count, top, reach, lean):
    order = jax.random.permutation(rng, count)
    heavy_load, ordinary = portions_of(count, rows * top, reach, lean, True), portions_of(count, rows * top, reach, lean, False)
    places = jnp.arange(count)

    def named(sizes, turn):
        used = int((sizes > 0).sum())
        fixed = max(1, used // 4)
        shifted = fixed + (places - fixed + turn * (used - fixed)) % max(1, count - fixed)
        return jnp.zeros((count,), jnp.int32).at[order[jnp.where(places < fixed, places, shifted)]].set(jnp.asarray(sizes, jnp.int32))

    sizes = jnp.where(number % 4 == 0, named(heavy_load, number // 4), named(ordinary, number - number // 4 - 1))
    mixed = jax.random.permutation(jax.random.fold_in(own, 3), count)
    donor, receiver = mixed[0:count // 2 * 2:2], mixed[1:count // 2 * 2:2]
    room = jnp.minimum(sizes[donor] - 1, reach - sizes[receiver]) // 2
    room = jnp.where((donor == order[0]) | (receiver == order[0]) | (sizes[receiver] == 0), 0, jnp.maximum(room, 0))
    shifted = jax.random.randint(jax.random.fold_in(own, 4), (count // 2,), 0, 1 << 20) % (room + 1)
    sizes = sizes.at[donor].add(-shifted).at[receiver].add(shifted)
    members = jnp.searchsorted(jnp.cumsum(sizes), jnp.arange(rows * top), side="right").astype(jnp.int32)
    listing = members.reshape(top, rows).T
    listing = listing[jax.random.permutation(jax.random.fold_in(own, 1), rows)]
    turn = jax.random.randint(jax.random.fold_in(own, 2), (rows, 1), 0, top)
    return jnp.take_along_axis(listing, (jnp.arange(top)[None, :] + turn) % top, axis=1)


def portions_of(count, total, most, skew, full):
    loads = [(1 << 20) // math.isqrt(standing ** skew) + 1 for standing in range(1, count + 1)]
    largest = most if full else min(most, max(-(-total // count), total * loads[0] // sum(loads)))
    least = 1 if total - largest >= count - 1 else 0
    holding, surplus = [largest] + [least] * (count - 1), total - largest - least * (count - 1)
    while surplus > 0:
        free = [i for i in range(1, count) if holding[i] < largest] or [i for i in range(1, count) if holding[i] < most]
        whole, budget = sum([loads[i] for i in free]), surplus
        for i in free:
            addition = min(most - holding[i], max(1, budget * loads[i] // whole), surplus)
            holding[i] = holding[i] + addition
            surplus = surplus - addition
    return np.array(holding)


def setup_inputs(seed: int = 0) -> dict:
    arg_keys = jax.random.split(jax.random.key(seed), 8)
    tokens = draw_tokens(jax.random.fold_in(arg_keys[7], 71), 0)
    cotangent = draw_cotangent(jax.random.fold_in(arg_keys[7], 71), 0)
    routes_keys = jax.random.split(jax.random.fold_in(arg_keys[2], 1), TOKENS // TOK_DEV)
    routes_turns = jax.random.permutation(jax.random.fold_in(arg_keys[2], 3), TOKENS // TOK_DEV)
    routes = jax.vmap(lambda own, number: routed_block(jax.random.fold_in(arg_keys[2], 2), own, number, TOK_DEV, EXPERTS, TOPK, CAP, 2))(routes_keys, routes_turns).reshape((TOKENS, TOPK))
    route_gates = jnp.clip(0.19921875 + 0.80078125 * jax.random.uniform(arg_keys[3], (TOKENS, TOPK), jnp.float32) ** block_levels(arg_keys[3], (TOKENS, TOPK), ((0, 32),), -0.2, 0.2), 0.19921875, 1.0).astype(jnp.bfloat16)
    example_ids = jax.vmap(lambda own: jnp.searchsorted(jnp.cumsum(ragged(own, EX_DEV, TOK_DEV, EX_MOST, 1)), jnp.arange(TOK_DEV), side="right"))(jax.random.split(arg_keys[4], N_EP)).reshape((N_EP, TOK_DEV)).astype(jnp.int32)
    gate_weight = draw_gate_weight(jax.random.fold_in(arg_keys[7], 71), 0)
    up_weight = draw_up_weight(jax.random.fold_in(arg_keys[7], 71), 0)
    return dict(tokens=tokens, cotangent=cotangent, routes=routes, route_gates=route_gates, example_ids=example_ids, gate_weight=gate_weight, up_weight=up_weight)


CLIP_SCALE = 0.6

def slot_table(route_rows, experts, capacity):
    row_count = route_rows.shape[0]
    flat_routes = route_rows.reshape(row_count, -1)
    expert_ids = jnp.arange(experts, dtype=jnp.int32)
    onehot = (flat_routes[:, :, None] == expert_ids[None, None, :]).astype(jnp.int32)
    slot_ranks = lax.optimization_barrier(jnp.sum((jnp.cumsum(onehot, axis=1) - 1) * onehot, axis=2))
    slot_ids = jnp.arange(capacity, dtype=jnp.int32)
    matches = (flat_routes[:, None, None, :] == expert_ids[None, :, None, None]) & (slot_ranks[:, None, None, :] == slot_ids[None, None, :, None])
    matches = matches.astype(jnp.int32)
    positions = jnp.arange(flat_routes.shape[1], dtype=jnp.int32)
    chosen = lax.optimization_barrier(jnp.sum(matches * positions[None, None, None, :], axis=3)).astype(jnp.int32)
    valid_mask = lax.optimization_barrier(jnp.sum(matches, axis=3)).astype(jnp.int32)
    return (chosen, valid_mask)

def reference(tokens, cotangent, routes, route_gates, example_ids, gate_weight, up_weight):
    clip_level = CLIP_SCALE * (FF * D) ** 0.5
    chosen, valid_mask = slot_table(routes.reshape(N_EP, TOK_DEV, TOPK), EXPERTS, CAP)
    token_of = (chosen // TOPK).reshape(N_EP, EXPERTS * CAP)
    keep_mask = valid_mask.astype(jnp.bfloat16)
    pick_rows = jax.vmap(lambda source, index: source[index])
    x_slots = pick_rows(tokens.reshape(N_EP, TOK_DEV, D), token_of).reshape(N_EP, EXPERTS, CAP, D) * keep_mask[..., None]
    c_slots = pick_rows(cotangent.reshape(N_EP, TOK_DEV, D), token_of).reshape(N_EP, EXPERTS, CAP, D) * keep_mask[..., None]
    slot_gate = pick_rows(route_gates.reshape(N_EP, TOK_DEV * TOPK), chosen.reshape(N_EP, -1)).reshape(N_EP, EXPERTS, CAP).astype(jnp.float32) * valid_mask.astype(jnp.float32)
    slot_example = pick_rows(example_ids, token_of).reshape(N_EP, EXPERTS, CAP)
    full_gate = gate_weight.reshape(EXPERTS, GROUP, D, FF // GROUP).transpose(0, 2, 1, 3).reshape(EXPERTS, D, FF)
    full_up = up_weight.reshape(EXPERTS, GROUP, D, FF // GROUP).transpose(0, 2, 1, 3).reshape(EXPERTS, D, FF)
    example_range = jnp.arange(EX_DEV, dtype=jnp.int32)

    def expert_pass(expert_items):
        expert_x, expert_c, weight_gate, weight_up, expert_gate, expert_example = expert_items
        flat_slots = expert_x.reshape(-1, D)
        gate_pre = jnp.dot(flat_slots, weight_gate, preferred_element_type=jnp.float32)
        up_pre = jnp.dot(flat_slots, weight_up, preferred_element_type=jnp.float32)
        hidden = (jax.nn.silu(gate_pre) * up_pre).astype(jnp.bfloat16)
        hidden_blocks = hidden.reshape(N_EP, CAP, FF).astype(jnp.float32)
        cot_blocks = expert_c.astype(jnp.float32)
        hidden_pairs = jnp.einsum('jah,jbh->jab', hidden_blocks, hidden_blocks, precision=lax.Precision.HIGHEST)
        cot_pairs = jnp.einsum('jad,jbd->jab', cot_blocks, cot_blocks, precision=lax.Precision.HIGHEST)
        same_example = (expert_example[:, :, None] == expert_example[:, None, :]).astype(jnp.float32)
        pair_terms = expert_gate[:, :, None] * expert_gate[:, None, :] * same_example * hidden_pairs * cot_pairs
        per_slot = lax.optimization_barrier(jnp.sum(pair_terms, axis=2))
        example_onehot = (expert_example[:, :, None] == example_range[None, None, :]).astype(jnp.float32)
        per_example = lax.optimization_barrier(jnp.sum(per_slot[:, :, None] * example_onehot, axis=1))
        return (hidden, per_example)
    hiddens, partial_norms = lax.map(expert_pass, (x_slots.transpose(1, 0, 2, 3), c_slots.transpose(1, 0, 2, 3), full_gate, full_up, slot_gate.transpose(1, 0, 2), slot_example.transpose(1, 0, 2)))
    norm_sq = lax.optimization_barrier(jnp.sum(partial_norms, axis=0)).reshape(EXAMPLES)
    norm_value = jnp.sqrt(norm_sq)
    norm_ratio = norm_value / clip_level
    factor = clip_level / jnp.maximum(norm_value, clip_level)
    example_onehot = (slot_example[..., None] == example_range).astype(jnp.float32)
    slot_factor = lax.optimization_barrier(jnp.sum(example_onehot * factor.reshape(N_EP, EX_DEV)[:, None, None, :], axis=3))
    scaled = ((slot_factor * slot_gate)[..., None] * c_slots.astype(jnp.float32)).astype(jnp.bfloat16)
    scaled = scaled.transpose(1, 0, 2, 3).reshape(EXPERTS, N_EP * CAP, D)

    def down_pass(expert_items):
        expert_hidden, expert_scaled = expert_items
        return jnp.dot(expert_hidden.T, expert_scaled, preferred_element_type=jnp.float32).astype(jnp.bfloat16)
    updates = lax.map(down_pass, (hiddens, scaled))
    clipped_sum = updates.reshape(EXPERTS * GROUP, FF // GROUP, D)
    return (clipped_sum, norm_ratio)
```

```python
import jax
import jax.numpy as jnp
from jax import lax
from jax.experimental import pallas as pl
from jax.experimental.pallas import tpu as pltpu
from jax.sharding import PartitionSpec as P

D = 6144
FF = 8192
CAP = 40
CLIP_SCALE = 0.6

NX = 4
NZ = 8
TP = 8
TOK = 128
SH = 768
UN = 256
CH = NX * CAP
SLOTS = NZ * CH
PAIR = 2 * CH
ORDER = (0, 1, 7, 2, 6, 3, 5, 4)

F32 = jnp.float32
BF16 = jnp.bfloat16
MESH = pl.DeviceIdType.MESH


def kernel(
    tok, cot, meta, wg_hbm, wu_hbm, out_hbm, ratio,
    tokraw, cotraw, metaraw, sel, xblk, cblk, rowblk, rowmeta,
    xf, cf, hf, wg, wu, accg, accu, outv,
    gcs, ghs, gcr, ghr, cold, colg, nz, nx, nt,
    wsem, lsem, osem,
    xs_s, xs_r, zs_s, zs_r, ys_s, ys_r, y2_s, y2_r, sb_s, sb_r,
    hy_s, hy_r, h2_s, h2_r, hb_s, hb_r, gs_s, gs_r, nz_s, nz_r, nx_s, nx_r, nt_s, nt_r,
):
    ep = lax.axis_index("ep")
    tp = lax.axis_index("tp")
    x, z = ep // NZ, ep % NZ
    y, core = tp // 2, tp % 2
    sib = y * 2 + (1 - core)
    right = ((y + 1) % 4) * 2 + core
    left = ((y + 3) % 4) * 2 + core
    far = ((y + 2) % 4) * 2 + core

    wcopies = [
        pltpu.make_async_copy(wg_hbm, wg, wsem.at[0]),
        pltpu.make_async_copy(wu_hbm, wu, wsem.at[1]),
    ]

    barrier = pltpu.get_barrier_semaphore()
    for d in range(1, NX):
        pl.semaphore_signal(barrier, inc=1, device_id=(((x + d) % NX) * NZ + z, tp), device_id_type=MESH)
    for d in range(1, NZ):
        pl.semaphore_signal(barrier, inc=1, device_id=(x * NZ + (z + d) % NZ, tp), device_id_type=MESH)
    for d in range(1, TP):
        pl.semaphore_signal(barrier, inc=1, device_id=(ep, (tp + d) % TP), device_id_type=MESH)
    pl.semaphore_wait(barrier, NX - 1 + NZ - 1 + TP - 1)

    sends = []

    def send(src, dst, ssem, rsem, dev):
        c = pltpu.make_async_remote_copy(
            src_ref=src, dst_ref=dst, send_sem=ssem, recv_sem=rsem, device_id=dev, device_id_type=MESH
        )
        c.start()
        sends.append(c)
        return c

    def arrived(dst, ssem, rsem):
        pltpu.make_async_remote_copy(
            src_ref=dst, dst_ref=dst, send_sem=ssem, recv_sem=rsem, device_id=(ep, sib), device_id_type=MESH
        ).wait_recv()

    def x_send(kind, src, buf):
        for d in range(1, NX):
            send(src, buf.at[x], xs_s.at[kind, d], xs_r.at[kind, d], (((x + d) % NX) * NZ + z, tp))

    def x_wait(kind, buf):
        for d in range(1, NX):
            arrived(buf.at[(x + NX - d) % NX], xs_s.at[kind, d], xs_r.at[kind, d])

    x_send(0, meta, metaraw)
    x_send(1, tok, tokraw)
    locals_ = [
        pltpu.make_async_copy(meta, metaraw.at[x], lsem.at[0]),
        pltpu.make_async_copy(tok, tokraw.at[x], lsem.at[1]),
        pltpu.make_async_copy(cot, cotraw.at[x], lsem.at[2]),
    ]
    for c in locals_:
        c.start()
    for c in wcopies:
        c.start()
    for c in locals_:
        c.wait()
    x_wait(0, metaraw)

    earlier = (
        lax.broadcasted_iota(jnp.int32, (TOK, TOK), 0) < lax.broadcasted_iota(jnp.int32, (TOK, TOK), 1)
    ).astype(BF16)
    members, gates, names = [], [], []
    for h in range(2):
        expert = (2 * x + h).astype(F32)
        for s in range(NX):
            m = metaraw[s]
            first = (m[0:1] == expert).astype(F32)
            second = (m[1:2] == expert).astype(F32)
            members.append(first + second)
            gates.append(first * m[2:3] + second * m[3:4])
            names.append(m[4:5] + (s * 4 * NZ + z * 4).astype(F32))
    member = jnp.concatenate(members, axis=0)
    rank = jnp.dot(member.astype(BF16), earlier, preferred_element_type=F32)
    rank = jnp.where(member > 0.5, rank, -1000.0)
    slot_iota = lax.broadcasted_iota(jnp.int32, (CH, TOK), 0).astype(F32)
    for h in range(2):
        for s in range(NX):
            place = rank[h * NX + s : h * NX + s + 1] + float(s * CAP)
            sel[h, :, s * TOK : (s + 1) * TOK] = (slot_iota == place).astype(F32).astype(BF16)
        values = jnp.concatenate(
            [
                jnp.concatenate(gates[h * NX : (h + 1) * NX], axis=1),
                jnp.concatenate(names[h * NX : (h + 1) * NX], axis=1),
                jnp.zeros((6, NX * TOK), F32),
            ],
            axis=0,
        )
        rows = lax.dot_general(
            values.astype(BF16), sel[h], (((1,), (1,)), ((), ())), preferred_element_type=F32
        )
        rowblk[h] = jnp.concatenate([rows, jnp.zeros((8, 256 - CH), F32)], axis=1)

    x_wait(1, tokraw)
    x_send(2, cot, cotraw)
    raw = tokraw[...].reshape(NX * TOK, SH)
    for h in range(2):
        xblk[h] = jnp.dot(sel[h], raw, preferred_element_type=F32).astype(BF16)

    def rows_of(k):
        return pl.ds(k * CH, CH)

    mine = z // 4
    for k in range(1, NZ):
        zd = (z + NZ - ORDER[k]) % NZ
        send(xblk.at[zd // 4], xf.at[tp, rows_of(k)], zs_s.at[0, k], zs_r.at[0, k], (x * NZ + zd, tp))
    for k in range(1, NZ):
        zd = (z + NZ - ORDER[k]) % NZ
        send(rowblk.at[zd // 4], rowmeta.at[z], zs_s.at[1, k], zs_r.at[1, k], (x * NZ + zd, tp))
    own = pltpu.make_async_copy(xblk.at[mine], xf.at[tp, rows_of(0)], lsem.at[3])
    own.start()
    rowmeta[z] = rowblk[mine]
    own.wait()

    def start_c():
        for k in range(1, NZ):
            zd = (z + NZ - ORDER[k]) % NZ
            send(cblk.at[zd // 4], cf.at[rows_of(k)], zs_s.at[2, k], zs_r.at[2, k], (x * NZ + zd, tp))

    def build_c():
        x_wait(2, cotraw)
        craw = cotraw[...].reshape(NX * TOK, SH)
        for h in range(2):
            cblk[h] = jnp.dot(sel[h], craw, preferred_element_type=F32).astype(BF16)
        cf[rows_of(0)] = cblk[mine]

    def spread(buf, rows, k, sy_s, sy_r, b_s, b_r):
        send(buf.at[tp, rows], buf.at[tp, rows], sy_s.at[0, k], sy_r.at[0, k], (ep, right))
        send(buf.at[tp, rows], buf.at[tp, rows], sy_s.at[1, k], sy_r.at[1, k], (ep, left))
        send(buf.at[tp, rows], buf.at[tp, rows], b_s.at[0, k], b_r.at[0, k], (ep, sib))

    def pass_on(buf, rows, k, sy_s, sy_r, f_s, f_r, b_s, b_r):
        arrived(buf.at[left, rows], sy_s.at[0, k], sy_r.at[0, k])
        if k % 2 == 0:
            send(buf.at[left, rows], buf.at[left, rows], f_s.at[k], f_r.at[k], (ep, right))
        send(buf.at[left, rows], buf.at[left, rows], b_s.at[1, k], b_r.at[1, k], (ep, sib))
        arrived(buf.at[right, rows], sy_s.at[1, k], sy_r.at[1, k])
        if k % 2 == 1:
            send(buf.at[right, rows], buf.at[right, rows], f_s.at[k], f_r.at[k], (ep, left))
        send(buf.at[right, rows], buf.at[right, rows], b_s.at[2, k], b_r.at[2, k], (ep, sib))

    def last_hop(buf, rows, k, f_s, f_r, b_s, b_r):
        arrived(buf.at[far, rows], f_s.at[k], f_r.at[k])
        send(buf.at[far, rows], buf.at[far, rows], b_s.at[3, k], b_r.at[3, k], (ep, sib))

    def from_sibling(buf, rows, k, b_s, b_r):
        for i, owner in enumerate((tp, left, right, far)):
            other = (owner // 2) * 2 + (1 - core)
            arrived(buf.at[other, rows], b_s.at[i, k], b_r.at[i, k])

    lane_iota = lax.broadcasted_iota(jnp.int32, (CAP, CH), 1)

    def compact(g):
        total = jnp.zeros((CAP, CH), F32)
        for b in range(NX):
            inside = (lane_iota >= b * CAP) & (lane_iota < (b + 1) * CAP)
            total = total + jnp.where(inside, g[b * CAP : (b + 1) * CAP], 0.0)
        return total

    def gram(block, which, k, out_buf, in_buf):
        g = compact(
            lax.dot_general(block, block, (((1,), (1,)), ((), ())), preferred_element_type=F32)
        )
        g = jnp.concatenate([g, jnp.zeros((CAP, 256 - CH), F32)], axis=1)
        owner = (z + ORDER[k]) % NZ
        out_buf[k] = g

        @pl.when(owner != tp)
        def _():
            pltpu.make_async_remote_copy(
                src_ref=out_buf.at[k], dst_ref=in_buf.at[tp], send_sem=gs_s.at[which, k],
                recv_sem=gs_r.at[which, tp], device_id=(ep, owner), device_id_type=MESH,
            ).start()

        @pl.when(owner == tp)
        def _():
            in_buf[tp] = g

    def gram_sent(which, k, out_buf, in_buf):
        owner = (z + ORDER[k]) % NZ

        @pl.when(owner != tp)
        def _():
            pltpu.make_async_remote_copy(
                src_ref=out_buf.at[k], dst_ref=in_buf.at[tp], send_sem=gs_s.at[which, k],
                recv_sem=gs_r.at[which, tp], device_id=(ep, owner), device_id_type=MESH,
            ).wait_send()

    def hidden_pair(p):
        rows = pl.ds(p * PAIR, PAIR)
        accg[...] = jnp.zeros_like(accg)
        accu[...] = jnp.zeros_like(accu)

        @pl.loop(0, TP)
        def _(j):
            depth = pl.ds(pl.multiple_of(j * SH, SH), SH)
            block = xf[j, rows, :]
            accg[...] += jnp.dot(block, wg[0, depth, :], preferred_element_type=F32)
            accu[...] += jnp.dot(block, wu[0, depth, :], preferred_element_type=F32)

        g = accg[...]
        h = (g / (1.0 + jnp.exp(-g)) * accu[...]).astype(BF16)
        hf[tp, rows, :] = h
        spread(hf, rows, p, hy_s, hy_r, hb_s, hb_r)
        for i in range(2):
            gram(h[i * CH : (i + 1) * CH], 1, 2 * p + i, ghs, ghr)

    for s in range(NZ + 5):
        if s < NZ:
            if s > 0:
                arrived(xf.at[tp, rows_of(s)], zs_s.at[0, s], zs_r.at[0, s])
            spread(xf, rows_of(s), s, ys_s, ys_r, sb_s, sb_r)
        if s == 1:
            build_c()
        if s == 4:
            start_c()
        k = s - 1
        if 0 <= k < NZ:
            pass_on(xf, rows_of(k), k, ys_s, ys_r, y2_s, y2_r, sb_s, sb_r)
        k = s - 2
        if 0 <= k < NZ:
            last_hop(xf, rows_of(k), k, y2_s, y2_r, sb_s, sb_r)
        if s >= 5 and s % 2 == 1 and (s - 5) // 2 < 4:
            p = (s - 5) // 2
            pass_on(hf, pl.ds(p * PAIR, PAIR), p, hy_s, hy_r, h2_s, h2_r, hb_s, hb_r)
        if s >= 6 and s % 2 == 0 and (s - 6) // 2 < 4:
            p = (s - 6) // 2
            last_hop(hf, pl.ds(p * PAIR, PAIR), p, h2_s, h2_r, hb_s, hb_r)
        k = s - 3
        if 0 <= k < NZ and k % 2 == 1:
            if k == 1:
                for c in wcopies:
                    c.wait()
            for q in (k - 1, k):
                from_sibling(xf, rows_of(q), q, sb_s, sb_r)
            hidden_pair(k // 2)

    eye = (
        lax.broadcasted_iota(jnp.int32, (CH, CH), 0) == lax.broadcasted_iota(jnp.int32, (CH, CH), 1)
    ).astype(BF16)
    for k in range(NZ):
        srcz = (z + ORDER[k]) % NZ
        if k > 0:
            arrived(cf.at[rows_of(k)], zs_s.at[2, k], zs_r.at[2, k])
            arrived(rowmeta.at[srcz], zs_s.at[1, k], zs_r.at[1, k])
        gram(cf[rows_of(k)], 0, k, gcs, gcr)
        rows = rowmeta[srcz][:, :CH]
        cols = lax.dot_general(eye, rows.astype(BF16), (((1,), (1,)), ((), ())), preferred_element_type=F32)
        colg[rows_of(k)] = cols[:, 0:1]
        cold[rows_of(k)] = cols[:, 1:2]

    for d in range(1, TP):
        j = (tp + d) % TP
        arrived(gcr.at[j], gs_s.at[0, 0], gs_r.at[0, j])
        arrived(ghr.at[j], gs_s.at[1, 0], gs_r.at[1, j])
    csum, hsum = gcr[0], ghr[0]
    for j in range(1, TP):
        csum = csum + gcr[j]
        hsum = hsum + ghr[j]
    rows = rowmeta[tp][:, :CH]
    cols = lax.dot_general(eye, rows.astype(BF16), (((1,), (1,)), ((), ())), preferred_element_type=F32)
    weight = jnp.where(cols[:, 1:2] == rows[1:2], cols[:, 0:1] * rows[0:1], 0.0)
    terms = compact(weight) * hsum[:, :CH] * csum[:, :CH]
    per_slot = jnp.sum(terms, axis=0, keepdims=True)
    belongs = (
        lax.broadcasted_iota(jnp.int32, (128, CH), 0).astype(F32) == rows[1:2]
    ).astype(F32)
    partial = lax.dot_general(
        jnp.broadcast_to(per_slot, (8, CH)), belongs, (((1,), (1,)), ((), ())),
        preferred_element_type=F32, precision=lax.Precision.HIGHEST,
    )

    def exchange(value, buf, count, me, device_of, ssem, rsem):
        buf[me] = value
        for d in range(1, count):
            send(buf.at[me], buf.at[me], ssem.at[d], rsem.at[d], device_of((me + d) % count))
        for d in range(1, count):
            arrived(buf.at[(me + count - d) % count], ssem.at[d], rsem.at[d])
        total = buf[0]
        for j in range(1, count):
            total = total + buf[j]
        return total

    total = exchange(partial, nz, NZ, z, lambda j: (x * NZ + j, tp), nz_s, nz_r)
    total = exchange(total, nx, NX, x, lambda j: (j * NZ + z, tp), nx_s, nx_r)
    total = exchange(total, nt, TP, tp, lambda j: (ep, j), nt_s, nt_r)

    clip_level = CLIP_SCALE * (FF * D) ** 0.5
    norm = jnp.sqrt(total)
    ratio[...] = norm / clip_level
    factor = (clip_level / jnp.maximum(norm, clip_level))[0:1]

    name_iota = lax.broadcasted_iota(jnp.int32, (CH, 128), 1).astype(F32)
    for k in range(NZ):
        hit = jnp.where(name_iota == cold[rows_of(k)], factor, 0.0)
        slot_factor = jnp.sum(hit, axis=1, keepdims=True)
        scale = slot_factor * colg[rows_of(k)]
        cf[rows_of(k)] = (scale * cf[rows_of(k)].astype(F32)).astype(BF16)

    for p in range(4):
        from_sibling(hf, pl.ds(p * PAIR, PAIR), p, hb_s, hb_r)

    @pl.loop(0, TP)
    def _(j):
        block = lax.dot_general(
            hf[j], cf[...], (((0,), (0,)), ((), ())), preferred_element_type=F32
        )
        outv[pl.ds(pl.multiple_of(j * UN, UN), UN), :] = block.astype(BF16)
        piece = pl.ds(pl.multiple_of(j * UN, UN), UN)
        pltpu.make_async_copy(outv.at[piece], out_hbm.at[0, piece], osem.at[j]).start()

    for k in range(NZ):
        gram_sent(0, k, gcs, gcr)
        gram_sent(1, k, ghs, ghr)
    for c in sends:
        c.wait_send()

    @pl.loop(0, TP)
    def _(j):
        piece = pl.ds(pl.multiple_of(j * UN, UN), UN)
        pltpu.make_async_copy(outv.at[piece], out_hbm.at[0, piece], osem.at[j]).wait()


def body(tokens, cotangent, routes, route_gates, example_ids, gate_weight, up_weight):
    meta = jnp.concatenate(
        [
            routes.T.astype(F32),
            route_gates.T.astype(F32),
            example_ids.astype(F32),
            jnp.zeros((3, TOK), F32),
        ],
        axis=0,
    )
    anywhere = pl.BlockSpec(memory_space=pl.ANY)
    dma = pltpu.SemaphoreType.DMA
    vm = pltpu.VMEM
    update, ratio = pl.pallas_call(
        kernel,
        out_shape=(
            jax.ShapeDtypeStruct((1, TP * UN, SH), BF16),
            jax.ShapeDtypeStruct((8, 128), F32),
        ),
        in_specs=[anywhere, anywhere, pl.BlockSpec(memory_space=vm), anywhere, anywhere],
        out_specs=(anywhere, pl.BlockSpec(memory_space=vm)),
        scratch_shapes=[
            vm((NX, TOK, SH), BF16),
            vm((NX, TOK, SH), BF16),
            vm((NX, 8, TOK), F32),
            vm((2, CH, NX * TOK), BF16),
            vm((2, CH, SH), BF16),
            vm((2, CH, SH), BF16),
            vm((2, 8, 256), F32),
            vm((NZ, 8, 256), F32),
            vm((TP, SLOTS, SH), BF16),
            vm((SLOTS, SH), BF16),
            vm((TP, SLOTS, UN), BF16),
            vm((1, D, UN), BF16),
            vm((1, D, UN), BF16),
            vm((PAIR, UN), F32),
            vm((PAIR, UN), F32),
            vm((TP * UN, SH), BF16),
            vm((NZ, CAP, 256), F32),
            vm((NZ, CAP, 256), F32),
            vm((TP, CAP, 256), F32),
            vm((TP, CAP, 256), F32),
            vm((SLOTS, 1), F32),
            vm((SLOTS, 1), F32),
            vm((NZ, 8, 128), F32),
            vm((NX, 8, 128), F32),
            vm((TP, 8, 128), F32),
            dma((2,)),
            dma((4,)),
            dma((TP,)),
            dma((3, NX)), dma((3, NX)),
            dma((3, NZ)), dma((3, NZ)),
            dma((2, NZ)), dma((2, NZ)),
            dma((NZ,)), dma((NZ,)),
            dma((4, NZ)), dma((4, NZ)),
            dma((2, 4)), dma((2, 4)),
            dma((4,)), dma((4,)),
            dma((4, 4)), dma((4, 4)),
            dma((2, NZ)), dma((2, TP)),
            dma((NZ,)), dma((NZ,)),
            dma((NX,)), dma((NX,)),
            dma((TP,)), dma((TP,)),
        ],
        compiler_params=pltpu.CompilerParams(
            collective_id=0, has_side_effects=True, vmem_limit_bytes=58 * 1024 * 1024
        ),
        cost_estimate=pl.CostEstimate(
            flops=12_000_000_000, bytes_accessed=10_000_000, transcendentals=327_680
        ),
        name="moe_clip",
    )(tokens, cotangent, meta, gate_weight, up_weight)
    return (update, ratio[0])


def solution(mesh):
    placed = (
        P("ep", "tp"),
        P("ep", "tp"),
        P("ep", None),
        P("ep", None),
        P("ep", None),
        P("ep", None, "tp"),
        P("ep", None, "tp"),
    )
    return jax.shard_map(
        body, mesh=mesh, in_specs=placed, out_specs=(P("ep", None, "tp"), P()), check_vma=False
    )
```

```python
import jax
import jax.numpy as jnp
from jax import lax
from jax.experimental import pallas as pl
from jax.experimental.pallas import tpu as pltpu
from jax.sharding import PartitionSpec as P

D = 6144
FF = 8192
CAP = 40
CLIP_SCALE = 0.6

NX = 4
NZ = 8
TP = 8
TOK = 128
SH = 768
UN = 256
CH = NX * CAP
SLOTS = NZ * CH
PAIR = 2 * CH

F32 = jnp.float32
BF16 = jnp.bfloat16
MESH = pl.DeviceIdType.MESH


def kernel(
    tok_hbm, cot_hbm, routes, gates, ids, wg_hbm, wu_hbm, out_hbm, ratio,
    tok, cot, metaraw, xs, cs, xraw, craw, sel, perm, xblk, cblk, rowblk, rowmeta,
    xf, cf, outs, hf, wg, wu, accg, accu, outv,
    gcs, gcr, hg, wc, cold, colg, nz, nx, nt,
    wsem, lsem, osem,
    xs_s, xs_r, zs_s, zs_r, ys_s, ys_r, y2_s, y2_r, sb_s, sb_r,
    hy_s, hy_r, h2_s, h2_r, hb_s, hb_r, gs_s, gs_r, wc_s, wc_r, nz_s, nz_r, nx_s, nx_r, nt_s, nt_r,
):
    ep = lax.axis_index("ep")
    tp = lax.axis_index("tp")
    x, z = ep // NZ, ep % NZ
    y, core = tp // 2, tp % 2
    sib = y * 2 + (1 - core)
    right = ((y + 1) % 4) * 2 + core
    left = ((y + 3) % 4) * 2 + core
    far = ((y + 2) % 4) * 2 + core
    q, mine = z % 4, z // 4

    tcopy = pltpu.make_async_copy(tok_hbm, tok, lsem.at[0])
    ccopy = pltpu.make_async_copy(cot_hbm, cot, lsem.at[1])
    wcopies = [
        pltpu.make_async_copy(wg_hbm, wg, wsem.at[0]),
        pltpu.make_async_copy(wu_hbm, wu, wsem.at[1]),
    ]
    tcopy.start()
    ccopy.start()

    barrier = pltpu.get_barrier_semaphore()
    for d in range(1, NX):
        pl.semaphore_signal(barrier, inc=1, device_id=(((x + d) % NX) * NZ + z, tp), device_id_type=MESH)
    for d in range(1, NZ):
        pl.semaphore_signal(barrier, inc=1, device_id=(x * NZ + (z + d) % NZ, tp), device_id_type=MESH)
    for d in range(1, TP):
        pl.semaphore_signal(barrier, inc=1, device_id=(ep, (tp + d) % TP), device_id_type=MESH)

    sends = []

    def send(src, dst, ssem, rsem, dev):
        c = pltpu.make_async_remote_copy(
            src_ref=src, dst_ref=dst, send_sem=ssem, recv_sem=rsem, device_id=dev, device_id_type=MESH
        )
        c.start()
        sends.append(c)
        return c

    def arrived(dst, ssem, rsem):
        pltpu.make_async_remote_copy(
            src_ref=dst, dst_ref=dst, send_sem=ssem, recv_sem=rsem, device_id=(ep, sib), device_id_type=MESH
        ).wait_recv()

    earlier = (
        lax.broadcasted_iota(jnp.int32, (TOK, TOK), 0) < lax.broadcasted_iota(jnp.int32, (TOK, TOK), 1)
    ).astype(BF16)
    r = routes[...].astype(F32)
    metaraw[x] = jnp.concatenate(
        [r, gates[...].astype(F32), ids[...].astype(F32), jnp.zeros((3, TOK), F32)], axis=0
    )
    expert_iota = lax.broadcasted_iota(jnp.int32, (8, TOK), 0).astype(F32)
    member = (expert_iota == r[0:1]).astype(F32) + (expert_iota == r[1:2]).astype(F32)
    rank = jnp.dot(member.astype(BF16), earlier, preferred_element_type=F32)
    rank = jnp.where(member > 0.5, rank, -1000.0)
    cap_iota = lax.broadcasted_iota(jnp.int32, (CAP, TOK), 0).astype(F32)
    own_sel = jnp.concatenate(
        [(cap_iota == rank[e : e + 1]).astype(F32) for e in range(8)], axis=0
    ).astype(BF16)
    tcopy.wait()
    xs[...] = jnp.dot(own_sel, tok[...], preferred_element_type=F32).astype(BF16).reshape(NX, 2 * CAP, SH)

    pl.semaphore_wait(barrier, NX - 1 + NZ - 1 + TP - 1)

    def x_send(kind, src, buf):
        for d in range(1, NX):
            xd = (x + d) % NX
            send(src(xd), buf.at[x], xs_s.at[kind, d], xs_r.at[kind, d], (xd * NZ + z, tp))

    def x_wait(kind, buf):
        for d in range(1, NX):
            arrived(buf.at[(x + NX - d) % NX], xs_s.at[kind, d], xs_r.at[kind, d])

    x_send(1, lambda xd: xs.at[xd], xraw)
    x_send(0, lambda xd: metaraw.at[x], metaraw)
    for c in wcopies:
        c.start()
    xraw[x] = xs[x]
    ccopy.wait()
    cs[...] = jnp.dot(own_sel, cot[...], preferred_element_type=F32).astype(BF16).reshape(NX, 2 * CAP, SH)

    craw[x] = cs[x]

    prow = lax.broadcasted_iota(jnp.int32, (CH, NX * 2 * CAP), 0)
    pcol = lax.broadcasted_iota(jnp.int32, (CH, NX * 2 * CAP), 1)
    source = sum(((prow >= b * CAP).astype(jnp.int32) for b in range(1, NX)), jnp.zeros_like(prow))
    for h in range(2):
        perm[h] = (pcol == prow + source * CAP + h * CAP).astype(F32).astype(BF16)

    x_wait(1, xraw)
    x_send(2, lambda xd: cs.at[xd], craw)
    raw = xraw[...].reshape(NX * 2 * CAP, SH)
    for h in range(2):
        xblk[h] = jnp.dot(perm[h], raw, preferred_element_type=F32).astype(BF16)

    def rows_of(k):
        return pl.ds(k * CH, CH)

    low = (q < 2).astype(jnp.int32)
    short = low * (q + 2) + (1 - low) * (5 - q)

    def place(qq, from_left, d):
        lo = (qq < 2).astype(jnp.int32)
        m = lo * (qq + 2) + (1 - lo) * (5 - qq)
        is_long = lo * (1 - from_left) + (1 - lo) * from_left
        within = (d <= m).astype(jnp.int32)
        return is_long * (within * (2 * d - 1) + (1 - within) * (m + d)) + (1 - is_long) * 2 * d

    from_left_at, dist_at, source_at = [0], [0], [z]
    for k in range(1, NZ):
        is_short = (k <= 2 * short).astype(jnp.int32) * (1 - k % 2)
        beyond = (k > 2 * short).astype(jnp.int32)
        d = is_short * (k // 2) + (1 - is_short) * (beyond * (k - short) + (1 - beyond) * ((k + 1) // 2))
        from_left = is_short * low + (1 - is_short) * (1 - low)
        from_left_at.append(from_left)
        dist_at.append(d)
        source_at.append((z + NZ + d * (1 - 2 * from_left)) % NZ)

    def z_copy(kind, src, dst, where, sidx, zd):
        return pltpu.make_async_remote_copy(
            src_ref=src, dst_ref=dst(where), send_sem=zs_s.at[kind, sidx], recv_sem=zs_r.at[kind, where],
            device_id=(x * NZ + zd, tp), device_id_type=MESH,
        )

    def z_starts(kind, blk, dst):
        to_right = (q >= 2).astype(jnp.int32)
        step = to_right * (4 - q) - (1 - to_right) * (q + 1)
        reach = to_right * (4 - q) + (1 - to_right) * (q + 1)
        entry = (1 - to_right) * 3
        return (
            (q < 3, lambda: z_copy(kind, blk.at[mine], dst, place(q + 1, 1, 1), 0, (z + 1) % NZ)),
            (q > 0, lambda: z_copy(kind, blk.at[mine], dst, place(q + 3 - 4, 0, 1), 8, (z + NZ - 1) % NZ)),
            (q >= 0, lambda: z_copy(kind, blk.at[1 - mine], dst, place(entry, to_right, reach), 9, (z + NZ + step) % NZ)),
        )

    def z_forward(kind, buf, k):
        fl, d = from_left_at[k], dist_at[k]
        go = fl * (q < 3).astype(jnp.int32) + (1 - fl) * (q > 0).astype(jnp.int32)
        qn = q + 2 * fl - 1
        return (
            go == 1,
            lambda: z_copy(kind, buf(k), buf, place(qn, fl, d + 1), k, (z + NZ + 2 * fl - 1) % NZ),
        )

    def x_rows(k):
        return xf.at[tp, pl.ds(pl.multiple_of(k * CH, CH), CH)]

    def c_rows(k):
        return cf.at[pl.ds(pl.multiple_of(k * CH, CH), CH)]

    def m_rows(k):
        return rowmeta.at[k]

    def start_if(pair):
        @pl.when(pair[0])
        def _():
            pair[1]().start()

    def sent_if(pair):
        @pl.when(pair[0])
        def _():
            pair[1]().wait_send()

    zsent = []

    def z_go(pair):
        start_if(pair)
        zsent.append(pair)

    for pair in z_starts(0, xblk, x_rows):
        z_go(pair)
    own = pltpu.make_async_copy(xblk.at[mine], xf.at[tp, rows_of(0)], lsem.at[3])
    own.start()

    def spread(buf, rows, k, sy_s, sy_r, b_s, b_r):
        send(buf.at[tp, rows], buf.at[tp, rows], sy_s.at[0, k], sy_r.at[0, k], (ep, right))
        send(buf.at[tp, rows], buf.at[tp, rows], sy_s.at[1, k], sy_r.at[1, k], (ep, left))
        send(buf.at[tp, rows], buf.at[tp, rows], b_s.at[0, k], b_r.at[0, k], (ep, sib))

    def pass_on(buf, rows, k, sy_s, sy_r, f_s, f_r, b_s, b_r):
        arrived(buf.at[left, rows], sy_s.at[0, k], sy_r.at[0, k])
        if k % 2 == 0:
            send(buf.at[left, rows], buf.at[left, rows], f_s.at[k], f_r.at[k], (ep, right))
        send(buf.at[left, rows], buf.at[left, rows], b_s.at[1, k], b_r.at[1, k], (ep, sib))
        arrived(buf.at[right, rows], sy_s.at[1, k], sy_r.at[1, k])
        if k % 2 == 1:
            send(buf.at[right, rows], buf.at[right, rows], f_s.at[k], f_r.at[k], (ep, left))
        send(buf.at[right, rows], buf.at[right, rows], b_s.at[2, k], b_r.at[2, k], (ep, sib))

    def last_hop(buf, rows, k, f_s, f_r, b_s, b_r):
        arrived(buf.at[far, rows], f_s.at[k], f_r.at[k])
        send(buf.at[far, rows], buf.at[far, rows], b_s.at[3, k], b_r.at[3, k], (ep, sib))

    def from_sibling(buf, rows, k, b_s, b_r):
        for i, owner in enumerate((tp, left, right, far)):
            other = (owner // 2) * 2 + (1 - core)
            arrived(buf.at[other, rows], b_s.at[i, k], b_r.at[i, k])

    own.wait()

    x_wait(0, metaraw)
    members, weights, names = [], [], []
    for h in range(2):
        expert = (2 * x + h).astype(F32)
        for s in range(NX):
            m = metaraw[s]
            first = (m[0:1] == expert).astype(F32)
            second = (m[1:2] == expert).astype(F32)
            members.append(first + second)
            weights.append(first * m[2:3] + second * m[3:4])
            names.append(m[4:5] + (s * 4 * NZ + z * 4).astype(F32))
    member = jnp.concatenate(members, axis=0)
    rank = jnp.dot(member.astype(BF16), earlier, preferred_element_type=F32)
    rank = jnp.where(member > 0.5, rank, -1000.0)
    slot_iota = lax.broadcasted_iota(jnp.int32, (CH, TOK), 0).astype(F32)
    for h in range(2):
        for s in range(NX):
            row = rank[h * NX + s : h * NX + s + 1] + float(s * CAP)
            sel[h, :, s * TOK : (s + 1) * TOK] = (slot_iota == row).astype(F32).astype(BF16)
        values = jnp.concatenate(
            [
                jnp.concatenate(weights[h * NX : (h + 1) * NX], axis=1),
                jnp.concatenate(names[h * NX : (h + 1) * NX], axis=1),
                jnp.zeros((6, NX * TOK), F32),
            ],
            axis=0,
        )
        rows = lax.dot_general(
            values.astype(BF16), sel[h], (((1,), (1,)), ((), ())), preferred_element_type=F32
        )
        rowblk[h] = jnp.concatenate([rows, jnp.zeros((8, 256 - CH), F32)], axis=1)
    for pair in z_starts(1, rowblk, m_rows):
        z_go(pair)
    rowmeta[0] = rowblk[mine]

    lane_iota = lax.broadcasted_iota(jnp.int32, (CAP, CH), 1)

    def compact(g):
        total = jnp.zeros((CAP, CH), F32)
        for b in range(NX):
            inside = (lane_iota >= b * CAP) & (lane_iota < (b + 1) * CAP)
            total = total + jnp.where(inside, g[b * CAP : (b + 1) * CAP], 0.0)
        return total

    def gram(block):
        return compact(
            lax.dot_general(block, block, (((1,), (1,)), ((), ())), preferred_element_type=F32)
        )

    def widen(g):
        return jnp.concatenate([g, jnp.zeros((CAP, 256 - CH), F32)], axis=1)

    eye = (
        lax.broadcasted_iota(jnp.int32, (CH, CH), 0) == lax.broadcasted_iota(jnp.int32, (CH, CH), 1)
    ).astype(BF16)

    def gram_copy(k):
        return (
            source_at[k] != tp,
            lambda: pltpu.make_async_remote_copy(
                src_ref=gcs.at[k], dst_ref=gcr.at[tp], send_sem=gs_s.at[k], recv_sem=gs_r.at[tp],
                device_id=(ep, source_at[k]), device_id_type=MESH,
            ),
        )

    def take_c(k):
        if k > 0:
            arrived(cf.at[rows_of(k)], zs_s.at[2, k], zs_r.at[2, k])
            z_go(z_forward(2, c_rows, k))
            arrived(rowmeta.at[k], zs_s.at[1, k], zs_r.at[1, k])
            z_go(z_forward(1, m_rows, k))
        g = widen(gram(cf[rows_of(k)]))
        gcs[k] = g
        start_if(gram_copy(k))

        @pl.when(source_at[k] == tp)
        def _():
            gcr[tp] = g

        rows = rowmeta[k][:, :CH]
        cols = lax.dot_general(eye, rows.astype(BF16), (((1,), (1,)), ((), ())), preferred_element_type=F32)
        colg[rows_of(k)] = cols[:, 0:1]
        cold[rows_of(k)] = cols[:, 1:2]

        @pl.when(source_at[k] == tp)
        def _():
            weight = jnp.where(cols[:, 1:2] == rows[1:2], cols[:, 0:1] * rows[0:1], 0.0)
            wc[tp] = widen(compact(weight))

    def build_c():
        x_wait(2, craw)
        raw = craw[...].reshape(NX * 2 * CAP, SH)
        for h in range(2):
            cblk[h] = jnp.dot(perm[h], raw, preferred_element_type=F32).astype(BF16)
        cf[rows_of(0)] = cblk[mine]

    def hidden_spread(p):
        spread(hf, pl.ds(p * PAIR, PAIR), p, hy_s, hy_r, hb_s, hb_r)

    def hidden_pass(p):
        pass_on(hf, pl.ds(p * PAIR, PAIR), p, hy_s, hy_r, h2_s, h2_r, hb_s, hb_r)

    def hidden_last(p):
        last_hop(hf, pl.ds(p * PAIR, PAIR), p, h2_s, h2_r, hb_s, hb_r)

    def hidden_chunk(k):
        rows = rows_of(k)
        accg[...] = jnp.zeros_like(accg)
        accu[...] = jnp.zeros_like(accu)

        @pl.loop(0, TP)
        def _(j):
            depth = pl.ds(pl.multiple_of(j * SH, SH), SH)
            block = xf[j, rows, :]
            accg[...] += jnp.dot(block, wg[0, depth, :], preferred_element_type=F32)
            accu[...] += jnp.dot(block, wu[0, depth, :], preferred_element_type=F32)

        g = accg[...]
        h = (g / (1.0 + jnp.exp(-g)) * accu[...]).astype(BF16)
        hf[tp, rows, :] = h
        if k == 5 or k == 7:
            hidden_spread(k // 2)
        hg[k] = gram(h)

    def share(k):
        per_slot = jnp.sum(wc[source_at[k]][:, :CH] * hg[k], axis=0, keepdims=True)
        belongs = (
            lax.broadcasted_iota(jnp.int32, (128, CH), 0).astype(F32) == rowmeta[k][1:2, :CH]
        ).astype(F32)
        return lax.dot_general(
            jnp.broadcast_to(per_slot, (8, CH)), belongs, (((1,), (1,)), ((), ())),
            preferred_element_type=F32, precision=lax.Precision.HIGHEST,
        )

    x_events = {0: (1,), 1: (2,), 2: (3,), 3: (4,), 4: (5,), 5: (6,), 6: (7,)}
    c_events = {3: (0,), 4: (1, 2), 5: (3,), 6: (4,), 7: (5,), 8: (6, 7)}
    partial = None
    for s in range(NZ + 3):
        if s == 0:
            spread(xf, rows_of(0), 0, ys_s, ys_r, sb_s, sb_r)
        for k in x_events.get(s, ()):
            arrived(xf.at[tp, rows_of(k)], zs_s.at[0, k], zs_r.at[0, k])
            z_go(z_forward(0, x_rows, k))
            spread(xf, rows_of(k), k, ys_s, ys_r, sb_s, sb_r)
        k = s - 1
        if 0 <= k < NZ:
            pass_on(xf, rows_of(k), k, ys_s, ys_r, y2_s, y2_r, sb_s, sb_r)
        if s == 1:
            build_c()
        if s == 2:
            for pair in z_starts(2, cblk, c_rows):
                z_go(pair)
        k = s - 2
        if 0 <= k < NZ:
            last_hop(xf, rows_of(k), k, y2_s, y2_r, sb_s, sb_r)
        if s == NZ:
            for p in range(2):
                hidden_spread(p)
        for k in c_events.get(s, ()):
            take_c(k)
        if s == 9:
            for d in range(1, TP):
                j = (tp + d) % TP
                arrived(gcr.at[j], gs_s.at[0], gs_r.at[j])
            csum = gcr[0]
            for j in range(1, TP):
                csum = csum + gcr[j]
            wc[tp] = wc[tp] * csum
            for d in range(1, TP):
                send(wc.at[tp], wc.at[tp], wc_s.at[d], wc_r.at[d], (ep, (tp + d) % TP))
        if s == 10:
            for d in range(1, TP):
                arrived(wc.at[(tp + TP - d) % TP], wc_s.at[d], wc_r.at[d])
            partial = share(0)
            for k in range(1, 7):
                partial = partial + share(k)
        k = s - 3
        if 0 <= k < NZ:
            if k == 0:
                for c in wcopies:
                    c.wait()
            from_sibling(xf, rows_of(k), k, sb_s, sb_r)
            hidden_chunk(k)

    partial = partial + share(7)

    def exchange_start(value, buf, count, me, device_of, ssem, rsem):
        buf[me] = value
        for d in range(1, count):
            send(buf.at[me], buf.at[me], ssem.at[d], rsem.at[d], device_of((me + d) % count))

    def exchange_end(buf, count, me, ssem, rsem):
        for d in range(1, count):
            arrived(buf.at[(me + count - d) % count], ssem.at[d], rsem.at[d])
        total = buf[0]
        for j in range(1, count):
            total = total + buf[j]
        return total

    exchange_start(partial, nz, NZ, z, lambda j: (x * NZ + j, tp), nz_s, nz_r)
    hidden_pass(0)
    total = exchange_end(nz, NZ, z, nz_s, nz_r)
    exchange_start(total, nx, NX, x, lambda j: (j * NZ + z, tp), nx_s, nx_r)
    hidden_pass(1)
    hidden_last(0)
    total = exchange_end(nx, NX, x, nx_s, nx_r)
    exchange_start(total, nt, TP, tp, lambda j: (ep, j), nt_s, nt_r)
    hidden_pass(2)
    hidden_last(1)
    hidden_pass(3)
    hidden_last(2)
    total = exchange_end(nt, TP, tp, nt_s, nt_r)

    clip_level = CLIP_SCALE * (FF * D) ** 0.5
    norm = jnp.sqrt(total[0:1])
    ratio[...] = norm / clip_level
    factor = clip_level / jnp.maximum(norm, clip_level)

    name_iota = lax.broadcasted_iota(jnp.int32, (CH, 128), 1).astype(F32)
    for k in range(NZ):
        hit = jnp.where(name_iota == cold[rows_of(k)], factor, 0.0)
        slot_factor = jnp.sum(hit, axis=1, keepdims=True)
        scale = slot_factor * colg[rows_of(k)]
        cs_k = (scale * cf[rows_of(k)].astype(F32)).astype(BF16)
        outs[rows_of(k)] = cs_k

    hidden_last(3)
    for p in range(4):
        from_sibling(hf, pl.ds(p * PAIR, PAIR), p, hb_s, hb_r)

    @pl.loop(0, TP)
    def _(j):
        block = lax.dot_general(
            hf[j], outs[...], (((0,), (0,)), ((), ())), preferred_element_type=F32
        )
        piece = pl.ds(pl.multiple_of(j * UN, UN), UN)
        outv[piece, :] = block.astype(BF16)
        pltpu.make_async_copy(outv.at[piece], out_hbm.at[0, piece], osem.at[j]).start()

    for k in range(NZ):
        sent_if(gram_copy(k))
    for pair in zsent:
        sent_if(pair)
    for c in sends:
        c.wait_send()

    @pl.loop(0, TP)
    def _(j):
        piece = pl.ds(pl.multiple_of(j * UN, UN), UN)
        pltpu.make_async_copy(outv.at[piece], out_hbm.at[0, piece], osem.at[j]).wait()


def body(tokens, cotangent, routes, route_gates, example_ids, gate_weight, up_weight):
    anywhere = pl.BlockSpec(memory_space=pl.ANY)
    dma = pltpu.SemaphoreType.DMA
    vm = pltpu.VMEM
    inside = pl.BlockSpec(memory_space=vm)
    update, ratio = pl.pallas_call(
        kernel,
        out_shape=(
            jax.ShapeDtypeStruct((1, TP * UN, SH), BF16),
            jax.ShapeDtypeStruct((1, 128), F32),
        ),
        in_specs=[anywhere, anywhere, inside, inside, inside, anywhere, anywhere],
        out_specs=(anywhere, inside),
        scratch_shapes=[
            vm((TOK, SH), BF16),
            vm((TOK, SH), BF16),
            vm((NX, 8, TOK), F32),
            vm((NX, 2 * CAP, SH), BF16),
            vm((NX, 2 * CAP, SH), BF16),
            vm((NX, 2 * CAP, SH), BF16),
            vm((NX, 2 * CAP, SH), BF16),
            vm((2, CH, NX * TOK), BF16),
            vm((2, CH, NX * 2 * CAP), BF16),
            vm((2, CH, SH), BF16),
            vm((2, CH, SH), BF16),
            vm((2, 8, 256), F32),
            vm((NZ, 8, 256), F32),
            vm((TP, SLOTS, SH), BF16),
            vm((SLOTS, SH), BF16),
            vm((SLOTS, SH), BF16),
            vm((TP, SLOTS, UN), BF16),
            vm((1, D, UN), BF16),
            vm((1, D, UN), BF16),
            vm((CH, UN), F32),
            vm((CH, UN), F32),
            vm((TP * UN, SH), BF16),
            vm((NZ, CAP, 256), F32),
            vm((TP, CAP, 256), F32),
            vm((NZ, CAP, CH), F32),
            vm((TP, CAP, 256), F32),
            vm((SLOTS, 1), F32),
            vm((SLOTS, 1), F32),
            vm((NZ, 8, 128), F32),
            vm((NX, 8, 128), F32),
            vm((TP, 8, 128), F32),
            dma((2,)),
            dma((4,)),
            dma((TP,)),
            dma((3, NX)), dma((3, NX)),
            dma((3, NZ + 2)), dma((3, NZ)),
            dma((2, NZ)), dma((2, NZ)),
            dma((NZ,)), dma((NZ,)),
            dma((4, NZ)), dma((4, NZ)),
            dma((2, 4)), dma((2, 4)),
            dma((4,)), dma((4,)),
            dma((4, 4)), dma((4, 4)),
            dma((NZ,)), dma((TP,)),
            dma((TP,)), dma((TP,)),
            dma((NZ,)), dma((NZ,)),
            dma((NX,)), dma((NX,)),
            dma((TP,)), dma((TP,)),
        ],
        compiler_params=pltpu.CompilerParams(
            collective_id=0, has_side_effects=True, vmem_limit_bytes=58 * 1024 * 1024
        ),
        cost_estimate=pl.CostEstimate(
            flops=12_000_000_000, bytes_accessed=10_000_000, transcendentals=327_680
        ),
        name="moe_clip",
    )(tokens, cotangent, routes.T, route_gates.T, example_ids, gate_weight, up_weight)
    return (update, ratio.reshape(128))


def solution(mesh):
    placed = (
        P("ep", "tp"),
        P("ep", "tp"),
        P("ep", None),
        P("ep", None),
        P("ep", None),
        P("ep", None, "tp"),
        P("ep", None, "tp"),
    )
    return jax.shard_map(
        body, mesh=mesh, in_specs=placed, out_specs=(P("ep", None, "tp"), P()), check_vma=False
    )
```

```python
import jax
import jax.numpy as jnp
from jax import lax
from jax.experimental import pallas as pl
from jax.experimental.pallas import tpu as pltpu
from jax.sharding import PartitionSpec as P

D = 6144
FF = 8192
CAP = 40
CLIP_SCALE = 0.6

NX = 4
NZ = 8
TP = 8
TOK = 128
SH = 768
UN = 256
CH = NX * CAP
SLOTS = NZ * CH
PAIR = 2 * CH

F32 = jnp.float32
BF16 = jnp.bfloat16
MESH = pl.DeviceIdType.MESH


def kernel(
    tok_hbm, cot_hbm, routes, gates, ids, wg_hbm, wu_hbm, out_hbm, ratio,
    tok, cot, metaraw, xs, cs, xraw, craw, sel, perm, xblk, cblk, rowblk, rowmeta,
    xf, cf, outs, hf, wg, wu, accg, accu, outv,
    gcs, gcr, wcs, hg, wc, cold, colg, nz, nx, nt,
    wsem, lsem, osem,
    xs_s, xs_r, zs_s, zs_r, ys_s, ys_r, y2_s, y2_r, sb_s, sb_r,
    hy_s, hy_r, h2_s, h2_r, hb_s, hb_r, gs_s, gs_r, wz_s, wz_r, wc_s, wc_r, wb_s, wb_r, nz_s, nz_r, nx_s, nx_r, nt_s, nt_r,
):
    ep = lax.axis_index("ep")
    tp = lax.axis_index("tp")
    x, z = ep // NZ, ep % NZ
    y, core = tp // 2, tp % 2
    sib = y * 2 + (1 - core)
    right = ((y + 1) % 4) * 2 + core
    left = ((y + 3) % 4) * 2 + core
    far = ((y + 2) % 4) * 2 + core
    q, mine = z % 4, z // 4

    tcopy = pltpu.make_async_copy(tok_hbm, tok, lsem.at[0])
    ccopy = pltpu.make_async_copy(cot_hbm, cot, lsem.at[1])
    wcopies = [
        pltpu.make_async_copy(wg_hbm, wg, wsem.at[0]),
        pltpu.make_async_copy(wu_hbm, wu, wsem.at[1]),
    ]
    tcopy.start()
    ccopy.start()

    barrier = pltpu.get_barrier_semaphore()
    for d in range(1, NX):
        pl.semaphore_signal(barrier, inc=1, device_id=(((x + d) % NX) * NZ + z, tp), device_id_type=MESH)
    for d in range(1, NZ):
        pl.semaphore_signal(barrier, inc=1, device_id=(x * NZ + (z + d) % NZ, tp), device_id_type=MESH)
    for d in range(1, TP):
        pl.semaphore_signal(barrier, inc=1, device_id=(ep, (tp + d) % TP), device_id_type=MESH)

    sends = []

    def send(src, dst, ssem, rsem, dev):
        c = pltpu.make_async_remote_copy(
            src_ref=src, dst_ref=dst, send_sem=ssem, recv_sem=rsem, device_id=dev, device_id_type=MESH
        )
        c.start()
        sends.append(c)
        return c

    def arrived(dst, ssem, rsem):
        pltpu.make_async_remote_copy(
            src_ref=dst, dst_ref=dst, send_sem=ssem, recv_sem=rsem, device_id=(ep, sib), device_id_type=MESH
        ).wait_recv()

    earlier = (
        lax.broadcasted_iota(jnp.int32, (TOK, TOK), 0) < lax.broadcasted_iota(jnp.int32, (TOK, TOK), 1)
    ).astype(BF16)
    r = routes[...].astype(F32)
    metaraw[x] = jnp.concatenate(
        [r, gates[...].astype(F32), ids[...].astype(F32), jnp.zeros((3, TOK), F32)], axis=0
    )
    expert_iota = lax.broadcasted_iota(jnp.int32, (8, TOK), 0).astype(F32)
    member = (expert_iota == r[0:1]).astype(F32) + (expert_iota == r[1:2]).astype(F32)
    rank = jnp.dot(member.astype(BF16), earlier, preferred_element_type=F32)
    rank = jnp.where(member > 0.5, rank, -1000.0)
    cap_iota = lax.broadcasted_iota(jnp.int32, (CAP, TOK), 0).astype(F32)
    own_sel = jnp.concatenate(
        [(cap_iota == rank[e : e + 1]).astype(F32) for e in range(8)], axis=0
    ).astype(BF16)
    tcopy.wait()
    xs[...] = jnp.dot(own_sel, tok[...], preferred_element_type=F32).astype(BF16).reshape(NX, 2 * CAP, SH)

    pl.semaphore_wait(barrier, NX - 1 + NZ - 1 + TP - 1)

    def x_send(kind, src, buf):
        for d in range(1, NX):
            xd = (x + d) % NX
            send(src(xd), buf.at[x], xs_s.at[kind, d], xs_r.at[kind, d], (xd * NZ + z, tp))

    def x_wait(kind, buf):
        for d in range(1, NX):
            arrived(buf.at[(x + NX - d) % NX], xs_s.at[kind, d], xs_r.at[kind, d])

    x_send(1, lambda xd: xs.at[xd], xraw)
    x_send(0, lambda xd: metaraw.at[x], metaraw)
    for c in wcopies:
        c.start()
    xraw[x] = xs[x]
    ccopy.wait()
    cs[...] = jnp.dot(own_sel, cot[...], preferred_element_type=F32).astype(BF16).reshape(NX, 2 * CAP, SH)

    craw[x] = cs[x]

    prow = lax.broadcasted_iota(jnp.int32, (CH, NX * 2 * CAP), 0)
    pcol = lax.broadcasted_iota(jnp.int32, (CH, NX * 2 * CAP), 1)
    source = sum(((prow >= b * CAP).astype(jnp.int32) for b in range(1, NX)), jnp.zeros_like(prow))
    for h in range(2):
        perm[h] = (pcol == prow + source * CAP + h * CAP).astype(F32).astype(BF16)

    x_wait(1, xraw)
    x_send(2, lambda xd: cs.at[xd], craw)
    raw = xraw[...].reshape(NX * 2 * CAP, SH)
    for h in range(2):
        xblk[h] = jnp.dot(perm[h], raw, preferred_element_type=F32).astype(BF16)

    def rows_of(k):
        return pl.ds(k * CH, CH)

    low = (q < 2).astype(jnp.int32)
    short = low * (q + 2) + (1 - low) * (5 - q)

    def place(qq, from_left, d):
        lo = (qq < 2).astype(jnp.int32)
        m = lo * (qq + 2) + (1 - lo) * (5 - qq)
        is_long = lo * (1 - from_left) + (1 - lo) * from_left
        within = (d <= m).astype(jnp.int32)
        return is_long * (within * (2 * d - 1) + (1 - within) * (m + d)) + (1 - is_long) * 2 * d

    from_left_at, dist_at, source_at = [0], [0], [z]
    for k in range(1, NZ):
        is_short = (k <= 2 * short).astype(jnp.int32) * (1 - k % 2)
        beyond = (k > 2 * short).astype(jnp.int32)
        d = is_short * (k // 2) + (1 - is_short) * (beyond * (k - short) + (1 - beyond) * ((k + 1) // 2))
        from_left = is_short * low + (1 - is_short) * (1 - low)
        from_left_at.append(from_left)
        dist_at.append(d)
        source_at.append((z + NZ + d * (1 - 2 * from_left)) % NZ)

    def z_copy(kind, src, dst, where, sidx, zd):
        return pltpu.make_async_remote_copy(
            src_ref=src, dst_ref=dst(where), send_sem=zs_s.at[kind, sidx], recv_sem=zs_r.at[kind, where],
            device_id=(x * NZ + zd, tp), device_id_type=MESH,
        )

    def z_starts(kind, blk, dst):
        to_right = (q >= 2).astype(jnp.int32)
        step = to_right * (4 - q) - (1 - to_right) * (q + 1)
        reach = to_right * (4 - q) + (1 - to_right) * (q + 1)
        entry = (1 - to_right) * 3
        return (
            (q < 3, lambda: z_copy(kind, blk.at[mine], dst, place(q + 1, 1, 1), 0, (z + 1) % NZ)),
            (q > 0, lambda: z_copy(kind, blk.at[mine], dst, place(q + 3 - 4, 0, 1), 8, (z + NZ - 1) % NZ)),
            (q >= 0, lambda: z_copy(kind, blk.at[1 - mine], dst, place(entry, to_right, reach), 9, (z + NZ + step) % NZ)),
        )

    def z_forward(kind, buf, k):
        fl, d = from_left_at[k], dist_at[k]
        go = fl * (q < 3).astype(jnp.int32) + (1 - fl) * (q > 0).astype(jnp.int32)
        qn = q + 2 * fl - 1
        return (
            go == 1,
            lambda: z_copy(kind, buf(k), buf, place(qn, fl, d + 1), k, (z + NZ + 2 * fl - 1) % NZ),
        )

    def x_rows(k):
        return xf.at[tp, pl.ds(pl.multiple_of(k * CH, CH), CH)]

    def c_rows(k):
        return cf.at[pl.ds(pl.multiple_of(k * CH, CH), CH)]

    def m_rows(k):
        return rowmeta.at[k]

    def start_if(pair):
        @pl.when(pair[0])
        def _():
            pair[1]().start()

    def sent_if(pair):
        @pl.when(pair[0])
        def _():
            pair[1]().wait_send()

    zsent = []

    def z_go(pair):
        start_if(pair)
        zsent.append(pair)

    for pair in z_starts(0, xblk, x_rows):
        z_go(pair)
    own = pltpu.make_async_copy(xblk.at[mine], xf.at[tp, rows_of(0)], lsem.at[3])
    own.start()

    def spread(buf, rows, k, sy_s, sy_r, b_s, b_r):
        send(buf.at[tp, rows], buf.at[tp, rows], sy_s.at[0, k], sy_r.at[0, k], (ep, right))
        send(buf.at[tp, rows], buf.at[tp, rows], sy_s.at[1, k], sy_r.at[1, k], (ep, left))
        send(buf.at[tp, rows], buf.at[tp, rows], b_s.at[0, k], b_r.at[0, k], (ep, sib))

    def pass_on(buf, rows, k, sy_s, sy_r, f_s, f_r, b_s, b_r):
        arrived(buf.at[left, rows], sy_s.at[0, k], sy_r.at[0, k])
        if k % 2 == 0:
            send(buf.at[left, rows], buf.at[left, rows], f_s.at[k], f_r.at[k], (ep, right))
        send(buf.at[left, rows], buf.at[left, rows], b_s.at[1, k], b_r.at[1, k], (ep, sib))
        arrived(buf.at[right, rows], sy_s.at[1, k], sy_r.at[1, k])
        if k % 2 == 1:
            send(buf.at[right, rows], buf.at[right, rows], f_s.at[k], f_r.at[k], (ep, left))
        send(buf.at[right, rows], buf.at[right, rows], b_s.at[2, k], b_r.at[2, k], (ep, sib))

    def last_hop(buf, rows, k, f_s, f_r, b_s, b_r):
        arrived(buf.at[far, rows], f_s.at[k], f_r.at[k])
        send(buf.at[far, rows], buf.at[far, rows], b_s.at[3, k], b_r.at[3, k], (ep, sib))

    def from_sibling(buf, rows, k, b_s, b_r):
        for i, owner in enumerate((tp, left, right, far)):
            other = (owner // 2) * 2 + (1 - core)
            arrived(buf.at[other, rows], b_s.at[i, k], b_r.at[i, k])

    own.wait()

    x_wait(0, metaraw)
    members, weights, names = [], [], []
    for h in range(2):
        expert = (2 * x + h).astype(F32)
        for s in range(NX):
            m = metaraw[s]
            first = (m[0:1] == expert).astype(F32)
            second = (m[1:2] == expert).astype(F32)
            members.append(first + second)
            weights.append(first * m[2:3] + second * m[3:4])
            names.append(m[4:5] + (s * 4 * NZ + z * 4).astype(F32))
    member = jnp.concatenate(members, axis=0)
    rank = jnp.dot(member.astype(BF16), earlier, preferred_element_type=F32)
    rank = jnp.where(member > 0.5, rank, -1000.0)
    slot_iota = lax.broadcasted_iota(jnp.int32, (CH, TOK), 0).astype(F32)
    for h in range(2):
        for s in range(NX):
            row = rank[h * NX + s : h * NX + s + 1] + float(s * CAP)
            sel[h, :, s * TOK : (s + 1) * TOK] = (slot_iota == row).astype(F32).astype(BF16)
        values = jnp.concatenate(
            [
                jnp.concatenate(weights[h * NX : (h + 1) * NX], axis=1),
                jnp.concatenate(names[h * NX : (h + 1) * NX], axis=1),
                jnp.zeros((6, NX * TOK), F32),
            ],
            axis=0,
        )
        rows = lax.dot_general(
            values.astype(BF16), sel[h], (((1,), (1,)), ((), ())), preferred_element_type=F32
        )
        rowblk[h] = jnp.concatenate([rows, jnp.zeros((8, 256 - CH), F32)], axis=1)
    for pair in z_starts(1, rowblk, m_rows):
        z_go(pair)
    rowmeta[0] = rowblk[mine]

    lane_iota = lax.broadcasted_iota(jnp.int32, (CAP, CH), 1)

    def compact(g):
        total = jnp.zeros((CAP, CH), F32)
        for b in range(NX):
            inside = (lane_iota >= b * CAP) & (lane_iota < (b + 1) * CAP)
            total = total + jnp.where(inside, g[b * CAP : (b + 1) * CAP], 0.0)
        return total

    def gram(block):
        return compact(
            lax.dot_general(block, block, (((1,), (1,)), ((), ())), preferred_element_type=F32)
        )

    def widen(g):
        return jnp.concatenate([g, jnp.zeros((CAP, 256 - CH), F32)], axis=1)

    eye = (
        lax.broadcasted_iota(jnp.int32, (CH, CH), 0) == lax.broadcasted_iota(jnp.int32, (CH, CH), 1)
    ).astype(BF16)

    def remote(src, dst, ssem, rsem, dev):
        return pltpu.make_async_remote_copy(
            src_ref=src, dst_ref=dst, send_sem=ssem, recv_sem=rsem, device_id=dev, device_id_type=MESH
        )

    def source_products():
        for h in range(2):
            gcs[h] = widen(gram(cblk[h]))
        z_go((tp != z, lambda: remote(gcs, gcr.at[tp], gs_s.at[0], gs_r.at[tp], (ep, z))))

    def owner_products():
        @pl.when(tp == z)
        def _():
            gcr[z] = gcs[...]
            for d in range(1, TP):
                arrived(gcr.at[(tp + d) % TP], gs_s.at[0], gs_r.at[(tp + d) % TP])
            for h in range(2):
                rows = rowblk[h][:, :CH]
                cols = lax.dot_general(
                    eye, rows.astype(BF16), (((1,), (1,)), ((), ())), preferred_element_type=F32
                )
                weight = jnp.where(cols[:, 1:2] == rows[1:2], cols[:, 0:1] * rows[0:1], 0.0)
                total = gcr[0, h]
                for j in range(1, TP):
                    total = total + gcr[j, h]
                wcs[h] = widen(compact(weight)) * total
            wc[z] = wcs[mine]

        for d in range(1, NZ):
            zd = (z + d) % NZ
            z_go((
                tp == z,
                lambda zd=zd, d=d: remote(wcs.at[zd // 4], wc.at[z], wz_s.at[d], wz_r.at[0], (x * NZ + zd, tp)),
            ))

    def gather_products():
        @pl.when(tp != z)
        def _():
            arrived(wc.at[tp], wz_s.at[1], wz_r.at[0])

        for i in (1, 2, 3):
            send(wc.at[tp], wc.at[tp], wc_s.at[i], wc_r.at[i], (ep, ((y + i) % 4) * 2 + core))
        send(wc.at[tp], wc.at[tp], wb_s.at[0], wb_r.at[0], (ep, sib))

    def take_c(k):
        if k > 0:
            arrived(cf.at[rows_of(k)], zs_s.at[2, k], zs_r.at[2, k])
            z_go(z_forward(2, c_rows, k))
            arrived(rowmeta.at[k], zs_s.at[1, k], zs_r.at[1, k])
            z_go(z_forward(1, m_rows, k))
        rows = rowmeta[k][:, :CH]
        cols = lax.dot_general(eye, rows.astype(BF16), (((1,), (1,)), ((), ())), preferred_element_type=F32)
        colg[rows_of(k)] = cols[:, 0:1]
        cold[rows_of(k)] = cols[:, 1:2]


    def build_c():
        x_wait(2, craw)
        raw = craw[...].reshape(NX * 2 * CAP, SH)
        for h in range(2):
            cblk[h] = jnp.dot(perm[h], raw, preferred_element_type=F32).astype(BF16)
        cf[rows_of(0)] = cblk[mine]

    def hidden_spread(p):
        spread(hf, pl.ds(p * PAIR, PAIR), p, hy_s, hy_r, hb_s, hb_r)

    def hidden_pass(p):
        pass_on(hf, pl.ds(p * PAIR, PAIR), p, hy_s, hy_r, h2_s, h2_r, hb_s, hb_r)

    def hidden_last(p):
        last_hop(hf, pl.ds(p * PAIR, PAIR), p, h2_s, h2_r, hb_s, hb_r)

    def hidden_chunk(k):
        rows = rows_of(k)
        accg[...] = jnp.zeros_like(accg)
        accu[...] = jnp.zeros_like(accu)

        @pl.loop(0, TP)
        def _(j):
            depth = pl.ds(pl.multiple_of(j * SH, SH), SH)
            block = xf[j, rows, :]
            accg[...] += jnp.dot(block, wg[0, depth, :], preferred_element_type=F32)
            accu[...] += jnp.dot(block, wu[0, depth, :], preferred_element_type=F32)

        g = accg[...]
        h = (g / (1.0 + jnp.exp(-g)) * accu[...]).astype(BF16)
        hf[tp, rows, :] = h
        if k == 5 or k == 7:
            hidden_spread(k // 2)
        hg[k] = gram(h)

    def shares():
        terms, named = [], []
        base = jnp.zeros((NZ, 128), jnp.int32)
        chunk_iota = lax.broadcasted_iota(jnp.int32, (NZ, 128), 0)
        for k in range(NZ):
            terms.append(jnp.sum(wc[source_at[k]][:, :CH] * hg[k], axis=0, keepdims=True))
            named.append(rowmeta[k][1:2, :CH])
            base = jnp.where(chunk_iota == k, source_at[k] * 4, base)
        term = jnp.concatenate(terms, axis=0)
        name = jnp.concatenate(named, axis=0)
        first = base[:, 0:1].astype(F32)
        lanes = lax.broadcasted_iota(jnp.int32, (NZ, 128), 1)
        total = jnp.zeros((NZ, 128), F32)
        for xs_ in range(NX):
            for ex in range(4):
                number = xs_ * 4 * NZ + ex
                one = jnp.sum(jnp.where(name == first + float(number), term, 0.0), axis=1, keepdims=True)
                total = total + jnp.where(lanes == base + number, one, 0.0)
        return jnp.broadcast_to(jnp.sum(total, axis=0, keepdims=True), (8, 128))

    x_events = {0: (1,), 1: (2,), 2: (3,), 3: (4,), 4: (5,), 5: (6,), 6: (7,)}
    c_events = {2: (0,), 3: (1,), 4: (2,), 5: (3,), 6: (4,), 7: (5,), 8: (6, 7)}
    for s in range(NZ + 3):
        if s == 0:
            spread(xf, rows_of(0), 0, ys_s, ys_r, sb_s, sb_r)
        for k in x_events.get(s, ()):
            arrived(xf.at[tp, rows_of(k)], zs_s.at[0, k], zs_r.at[0, k])
            z_go(z_forward(0, x_rows, k))
            spread(xf, rows_of(k), k, ys_s, ys_r, sb_s, sb_r)
        k = s - 1
        if 0 <= k < NZ:
            pass_on(xf, rows_of(k), k, ys_s, ys_r, y2_s, y2_r, sb_s, sb_r)
        if s == 0:
            build_c()
            source_products()
        if s == 1:
            for pair in z_starts(2, cblk, c_rows):
                z_go(pair)
        k = s - 2
        if 0 <= k < NZ:
            last_hop(xf, rows_of(k), k, y2_s, y2_r, sb_s, sb_r)
        if s == NZ:
            for p in range(2):
                hidden_spread(p)
        for k in c_events.get(s, ()):
            take_c(k)
        if s == 3:
            owner_products()
        if s == 5:
            gather_products()
        if s == 7:
            for i in (1, 2, 3):
                j = ((y + i) % 4) * 2 + core
                arrived(wc.at[j], wc_s.at[i], wc_r.at[4 - i])
                send(wc.at[j], wc.at[j], wb_s.at[i], wb_r.at[4 - i], (ep, sib))
        if s == 10:
            hidden_pass(0)
        k = s - 3
        if 0 <= k < NZ:
            if k == 0:
                for c in wcopies:
                    c.wait()
            from_sibling(xf, rows_of(k), k, sb_s, sb_r)
            hidden_chunk(k)

    for i in range(4):
        arrived(wc.at[((y + i) % 4) * 2 + 1 - core], wb_s.at[i], wb_r.at[(4 - i) % 4])
    partial = shares()

    def exchange_start(value, buf, count, me, device_of, ssem, rsem):
        buf[me] = value
        for d in range(1, count):
            send(buf.at[me], buf.at[me], ssem.at[d], rsem.at[d], device_of((me + d) % count))

    def exchange_end(buf, count, me, ssem, rsem):
        for d in range(1, count):
            arrived(buf.at[(me + count - d) % count], ssem.at[d], rsem.at[d])
        total = buf[0]
        for j in range(1, count):
            total = total + buf[j]
        return total

    exchange_start(partial, nz, NZ, z, lambda j: (x * NZ + j, tp), nz_s, nz_r)
    hidden_pass(1)
    total = exchange_end(nz, NZ, z, nz_s, nz_r)
    exchange_start(total, nx, NX, x, lambda j: (j * NZ + z, tp), nx_s, nx_r)
    hidden_last(0)
    hidden_pass(2)
    total = exchange_end(nx, NX, x, nx_s, nx_r)
    exchange_start(total, nt, TP, tp, lambda j: (ep, j), nt_s, nt_r)
    hidden_last(1)
    hidden_pass(3)
    hidden_last(2)
    total = exchange_end(nt, TP, tp, nt_s, nt_r)

    clip_level = CLIP_SCALE * (FF * D) ** 0.5
    norm = jnp.sqrt(total[0:1])
    ratio[...] = norm / clip_level
    factor = clip_level / jnp.maximum(norm, clip_level)

    name_iota = lax.broadcasted_iota(jnp.int32, (CH, 128), 1).astype(F32)
    for k in range(NZ):
        hit = jnp.where(name_iota == cold[rows_of(k)], factor, 0.0)
        slot_factor = jnp.sum(hit, axis=1, keepdims=True)
        scale = slot_factor * colg[rows_of(k)]
        cs_k = (scale * cf[rows_of(k)].astype(F32)).astype(BF16)
        outs[rows_of(k)] = cs_k

    hidden_last(3)
    for p in range(4):
        from_sibling(hf, pl.ds(p * PAIR, PAIR), p, hb_s, hb_r)

    @pl.loop(0, TP)
    def _(j):
        block = lax.dot_general(
            hf[j], outs[...], (((0,), (0,)), ((), ())), preferred_element_type=F32
        )
        piece = pl.ds(pl.multiple_of(j * UN, UN), UN)
        outv[piece, :] = block.astype(BF16)
        pltpu.make_async_copy(outv.at[piece], out_hbm.at[0, piece], osem.at[j]).start()

    for pair in zsent:
        sent_if(pair)
    for c in sends:
        c.wait_send()

    @pl.loop(0, TP)
    def _(j):
        piece = pl.ds(pl.multiple_of(j * UN, UN), UN)
        pltpu.make_async_copy(outv.at[piece], out_hbm.at[0, piece], osem.at[j]).wait()


def body(tokens, cotangent, routes, route_gates, example_ids, gate_weight, up_weight):
    anywhere = pl.BlockSpec(memory_space=pl.ANY)
    dma = pltpu.SemaphoreType.DMA
    vm = pltpu.VMEM
    inside = pl.BlockSpec(memory_space=vm)
    update, ratio = pl.pallas_call(
        kernel,
        out_shape=(
            jax.ShapeDtypeStruct((1, TP * UN, SH), BF16),
            jax.ShapeDtypeStruct((1, 128), F32),
        ),
        in_specs=[anywhere, anywhere, inside, inside, inside, anywhere, anywhere],
        out_specs=(anywhere, inside),
        scratch_shapes=[
            vm((TOK, SH), BF16),
            vm((TOK, SH), BF16),
            vm((NX, 8, TOK), F32),
            vm((NX, 2 * CAP, SH), BF16),
            vm((NX, 2 * CAP, SH), BF16),
            vm((NX, 2 * CAP, SH), BF16),
            vm((NX, 2 * CAP, SH), BF16),
            vm((2, CH, NX * TOK), BF16),
            vm((2, CH, NX * 2 * CAP), BF16),
            vm((2, CH, SH), BF16),
            vm((2, CH, SH), BF16),
            vm((2, 8, 256), F32),
            vm((NZ, 8, 256), F32),
            vm((TP, SLOTS, SH), BF16),
            vm((SLOTS, SH), BF16),
            vm((SLOTS, SH), BF16),
            vm((TP, SLOTS, UN), BF16),
            vm((1, D, UN), BF16),
            vm((1, D, UN), BF16),
            vm((CH, UN), F32),
            vm((CH, UN), F32),
            vm((TP * UN, SH), BF16),
            vm((2, CAP, 256), F32),
            vm((TP, 2, CAP, 256), F32),
            vm((2, CAP, 256), F32),
            vm((NZ, CAP, CH), F32),
            vm((TP, CAP, 256), F32),
            vm((SLOTS, 1), F32),
            vm((SLOTS, 1), F32),
            vm((NZ, 8, 128), F32),
            vm((NX, 8, 128), F32),
            vm((TP, 8, 128), F32),
            dma((2,)),
            dma((4,)),
            dma((TP,)),
            dma((3, NX)), dma((3, NX)),
            dma((3, NZ + 2)), dma((3, NZ)),
            dma((2, NZ)), dma((2, NZ)),
            dma((NZ,)), dma((NZ,)),
            dma((4, NZ)), dma((4, NZ)),
            dma((2, 4)), dma((2, 4)),
            dma((4,)), dma((4,)),
            dma((4, 4)), dma((4, 4)),
            dma((1,)), dma((TP,)),
            dma((NZ,)), dma((1,)),
            dma((4,)), dma((4,)),
            dma((4,)), dma((4,)),
            dma((NZ,)), dma((NZ,)),
            dma((NX,)), dma((NX,)),
            dma((TP,)), dma((TP,)),
        ],
        compiler_params=pltpu.CompilerParams(
            collective_id=0, has_side_effects=True, vmem_limit_bytes=58 * 1024 * 1024
        ),
        cost_estimate=pl.CostEstimate(
            flops=12_000_000_000, bytes_accessed=10_000_000, transcendentals=327_680
        ),
        name="moe_clip",
    )(tokens, cotangent, routes.T, route_gates.T, example_ids, gate_weight, up_weight)
    return (update, ratio.reshape(128))


def solution(mesh):
    placed = (
        P("ep", "tp"),
        P("ep", "tp"),
        P("ep", None),
        P("ep", None),
        P("ep", None),
        P("ep", None, "tp"),
        P("ep", None, "tp"),
    )
    return jax.shard_map(
        body, mesh=mesh, in_specs=placed, out_specs=(P("ep", None, "tp"), P()), check_vma=False
    )
```

```python
import jax
import jax.numpy as jnp
from jax import lax
from jax.experimental import pallas as pl
from jax.experimental.pallas import tpu as pltpu
from jax.sharding import PartitionSpec as P

D = 6144
FF = 8192
CAP = 40
CLIP_SCALE = 0.6

NX = 4
NZ = 8
TP = 8
TOK = 128
SH = 768
UN = 256
CH = NX * CAP
SLOTS = NZ * CH
PAIR = 2 * CH

F32 = jnp.float32
BF16 = jnp.bfloat16
MESH = pl.DeviceIdType.MESH


def kernel(
    tok_hbm, cot_hbm, routes, gates, ids, wg_hbm, wu_hbm, out_hbm, ratio,
    tok, cot, metaraw, xs, cs, xraw, craw, sel, perm, xblk, cblk, rowblk, rowmeta,
    xf, cf, outs, hf, wg, wu, accg, accu, outv,
    gcs, gcr, wcs, hg, wc, cold, colg, nz, nx, nt,
    wsem, lsem, osem,
    xs_s, xs_r, zs_s, zs_r, ys_s, ys_r, y2_s, y2_r, sb_s, sb_r,
    hy_s, hy_r, h2_s, h2_r, hb_s, hb_r, gs_s, gs_r, wz_s, wz_r, wc_s, wc_r, wb_s, wb_r, nz_s, nz_r, nx_s, nx_r, nt_s, nt_r,
):
    ep = lax.axis_index("ep")
    tp = lax.axis_index("tp")
    x, z = ep // NZ, ep % NZ
    y, core = tp // 2, tp % 2
    sib = y * 2 + (1 - core)
    right = ((y + 1) % 4) * 2 + core
    left = ((y + 3) % 4) * 2 + core
    far = ((y + 2) % 4) * 2 + core
    q, mine = z % 4, z // 4

    tcopy = pltpu.make_async_copy(tok_hbm, tok, lsem.at[0])
    ccopy = pltpu.make_async_copy(cot_hbm, cot, lsem.at[1])
    wcopies = [
        pltpu.make_async_copy(wg_hbm, wg, wsem.at[0]),
        pltpu.make_async_copy(wu_hbm, wu, wsem.at[1]),
    ]
    tcopy.start()
    ccopy.start()

    barrier = pltpu.get_barrier_semaphore()
    for d in range(1, NX):
        pl.semaphore_signal(barrier, inc=1, device_id=(((x + d) % NX) * NZ + z, tp), device_id_type=MESH)
    for d in range(1, NZ):
        pl.semaphore_signal(barrier, inc=1, device_id=(x * NZ + (z + d) % NZ, tp), device_id_type=MESH)
    for d in range(1, TP):
        pl.semaphore_signal(barrier, inc=1, device_id=(ep, (tp + d) % TP), device_id_type=MESH)

    sends = []

    def send(src, dst, ssem, rsem, dev):
        c = pltpu.make_async_remote_copy(
            src_ref=src, dst_ref=dst, send_sem=ssem, recv_sem=rsem, device_id=dev, device_id_type=MESH
        )
        c.start()
        sends.append(c)
        return c

    def arrived(dst, ssem, rsem):
        pltpu.make_async_remote_copy(
            src_ref=dst, dst_ref=dst, send_sem=ssem, recv_sem=rsem, device_id=(ep, sib), device_id_type=MESH
        ).wait_recv()

    earlier = (
        lax.broadcasted_iota(jnp.int32, (TOK, TOK), 0) < lax.broadcasted_iota(jnp.int32, (TOK, TOK), 1)
    ).astype(BF16)
    r = routes[...].astype(F32)
    metaraw[x] = jnp.concatenate(
        [r, gates[...].astype(F32), ids[...].astype(F32), jnp.zeros((3, TOK), F32)], axis=0
    )
    expert_iota = lax.broadcasted_iota(jnp.int32, (8, TOK), 0).astype(F32)
    member = (expert_iota == r[0:1]).astype(F32) + (expert_iota == r[1:2]).astype(F32)
    rank = jnp.dot(member.astype(BF16), earlier, preferred_element_type=F32)
    rank = jnp.where(member > 0.5, rank, -1000.0)
    cap_iota = lax.broadcasted_iota(jnp.int32, (CAP, TOK), 0).astype(F32)
    own_sel = jnp.concatenate(
        [(cap_iota == rank[e : e + 1]).astype(F32) for e in range(8)], axis=0
    ).astype(BF16)
    tcopy.wait()
    xs[...] = jnp.dot(own_sel, tok[...], preferred_element_type=F32).astype(BF16).reshape(NX, 2 * CAP, SH)

    pl.semaphore_wait(barrier, NX - 1 + NZ - 1 + TP - 1)

    def x_send(kind, src, buf):
        for d in range(1, NX):
            xd = (x + d) % NX
            send(src(xd), buf.at[x], xs_s.at[kind, d], xs_r.at[kind, d], (xd * NZ + z, tp))

    def x_wait(kind, buf):
        for d in range(1, NX):
            arrived(buf.at[(x + NX - d) % NX], xs_s.at[kind, d], xs_r.at[kind, d])

    x_send(1, lambda xd: xs.at[xd], xraw)
    x_send(0, lambda xd: metaraw.at[x], metaraw)
    for c in wcopies:
        c.start()
    xraw[x] = xs[x]
    ccopy.wait()
    cs[...] = jnp.dot(own_sel, cot[...], preferred_element_type=F32).astype(BF16).reshape(NX, 2 * CAP, SH)

    craw[x] = cs[x]

    prow = lax.broadcasted_iota(jnp.int32, (CH, NX * 2 * CAP), 0)
    pcol = lax.broadcasted_iota(jnp.int32, (CH, NX * 2 * CAP), 1)
    source = sum(((prow >= b * CAP).astype(jnp.int32) for b in range(1, NX)), jnp.zeros_like(prow))
    for h in range(2):
        perm[h] = (pcol == prow + source * CAP + h * CAP).astype(F32).astype(BF16)

    x_wait(1, xraw)
    x_send(2, lambda xd: cs.at[xd], craw)
    raw = xraw[...].reshape(NX * 2 * CAP, SH)
    for h in range(2):
        xblk[h] = jnp.dot(perm[h], raw, preferred_element_type=F32).astype(BF16)

    def rows_of(k):
        return pl.ds(k * CH, CH)

    low = (q < 2).astype(jnp.int32)
    short = low * (q + 2) + (1 - low) * (5 - q)

    def place(qq, from_left, d):
        lo = (qq < 2).astype(jnp.int32)
        m = lo * (qq + 2) + (1 - lo) * (5 - qq)
        is_long = lo * (1 - from_left) + (1 - lo) * from_left
        within = (d <= m).astype(jnp.int32)
        return is_long * (within * (2 * d - 1) + (1 - within) * (m + d)) + (1 - is_long) * 2 * d

    from_left_at, dist_at, source_at = [0], [0], [z]
    for k in range(1, NZ):
        is_short = (k <= 2 * short).astype(jnp.int32) * (1 - k % 2)
        beyond = (k > 2 * short).astype(jnp.int32)
        d = is_short * (k // 2) + (1 - is_short) * (beyond * (k - short) + (1 - beyond) * ((k + 1) // 2))
        from_left = is_short * low + (1 - is_short) * (1 - low)
        from_left_at.append(from_left)
        dist_at.append(d)
        source_at.append((z + NZ + d * (1 - 2 * from_left)) % NZ)

    def z_copy(kind, src, dst, where, sidx, zd):
        return pltpu.make_async_remote_copy(
            src_ref=src, dst_ref=dst(where), send_sem=zs_s.at[kind, sidx], recv_sem=zs_r.at[kind, where],
            device_id=(x * NZ + zd, tp), device_id_type=MESH,
        )

    def z_starts(kind, blk, dst):
        to_right = (q >= 2).astype(jnp.int32)
        step = to_right * (4 - q) - (1 - to_right) * (q + 1)
        reach = to_right * (4 - q) + (1 - to_right) * (q + 1)
        entry = (1 - to_right) * 3
        return (
            (q < 3, lambda: z_copy(kind, blk.at[mine], dst, place(q + 1, 1, 1), 0, (z + 1) % NZ)),
            (q > 0, lambda: z_copy(kind, blk.at[mine], dst, place(q + 3 - 4, 0, 1), 8, (z + NZ - 1) % NZ)),
            (q >= 0, lambda: z_copy(kind, blk.at[1 - mine], dst, place(entry, to_right, reach), 9, (z + NZ + step) % NZ)),
        )

    def z_forward(kind, buf, k):
        fl, d = from_left_at[k], dist_at[k]
        go = fl * (q < 3).astype(jnp.int32) + (1 - fl) * (q > 0).astype(jnp.int32)
        qn = q + 2 * fl - 1
        return (
            go == 1,
            lambda: z_copy(kind, buf(k), buf, place(qn, fl, d + 1), k, (z + NZ + 2 * fl - 1) % NZ),
        )

    def x_rows(k):
        return xf.at[tp, pl.ds(pl.multiple_of(k * CH, CH), CH)]

    def c_rows(k):
        return cf.at[pl.ds(pl.multiple_of(k * CH, CH), CH)]

    def m_rows(k):
        return rowmeta.at[k]

    def start_if(pair):
        @pl.when(pair[0])
        def _():
            pair[1]().start()

    def sent_if(pair):
        @pl.when(pair[0])
        def _():
            pair[1]().wait_send()

    zsent = []

    def z_go(pair):
        start_if(pair)
        zsent.append(pair)

    for pair in z_starts(0, xblk, x_rows):
        z_go(pair)
    own = pltpu.make_async_copy(xblk.at[mine], xf.at[tp, rows_of(0)], lsem.at[3])
    own.start()

    def spread(buf, rows, k, sy_s, sy_r, b_s, b_r):
        send(buf.at[tp, rows], buf.at[tp, rows], sy_s.at[0, k], sy_r.at[0, k], (ep, right))
        send(buf.at[tp, rows], buf.at[tp, rows], sy_s.at[1, k], sy_r.at[1, k], (ep, left))
        send(buf.at[tp, rows], buf.at[tp, rows], b_s.at[0, k], b_r.at[0, k], (ep, sib))

    def pass_on(buf, rows, k, sy_s, sy_r, f_s, f_r, b_s, b_r):
        arrived(buf.at[left, rows], sy_s.at[0, k], sy_r.at[0, k])
        if k % 2 == 0:
            send(buf.at[left, rows], buf.at[left, rows], f_s.at[k], f_r.at[k], (ep, right))
        send(buf.at[left, rows], buf.at[left, rows], b_s.at[1, k], b_r.at[1, k], (ep, sib))
        arrived(buf.at[right, rows], sy_s.at[1, k], sy_r.at[1, k])
        if k % 2 == 1:
            send(buf.at[right, rows], buf.at[right, rows], f_s.at[k], f_r.at[k], (ep, left))
        send(buf.at[right, rows], buf.at[right, rows], b_s.at[2, k], b_r.at[2, k], (ep, sib))

    def last_hop(buf, rows, k, f_s, f_r, b_s, b_r):
        arrived(buf.at[far, rows], f_s.at[k], f_r.at[k])
        send(buf.at[far, rows], buf.at[far, rows], b_s.at[3, k], b_r.at[3, k], (ep, sib))

    def from_sibling(buf, rows, k, b_s, b_r):
        for i, owner in enumerate((tp, left, right, far)):
            other = (owner // 2) * 2 + (1 - core)
            arrived(buf.at[other, rows], b_s.at[i, k], b_r.at[i, k])

    own.wait()

    x_wait(0, metaraw)
    members, weights, names = [], [], []
    for h in range(2):
        expert = (2 * x + h).astype(F32)
        for s in range(NX):
            m = metaraw[s]
            first = (m[0:1] == expert).astype(F32)
            second = (m[1:2] == expert).astype(F32)
            members.append(first + second)
            weights.append(first * m[2:3] + second * m[3:4])
            names.append(m[4:5] + (s * 4 * NZ + z * 4).astype(F32))
    member = jnp.concatenate(members, axis=0)
    rank = jnp.dot(member.astype(BF16), earlier, preferred_element_type=F32)
    rank = jnp.where(member > 0.5, rank, -1000.0)
    slot_iota = lax.broadcasted_iota(jnp.int32, (CH, TOK), 0).astype(F32)
    for h in range(2):
        for s in range(NX):
            row = rank[h * NX + s : h * NX + s + 1] + float(s * CAP)
            sel[h, :, s * TOK : (s + 1) * TOK] = (slot_iota == row).astype(F32).astype(BF16)
        values = jnp.concatenate(
            [
                jnp.concatenate(weights[h * NX : (h + 1) * NX], axis=1),
                jnp.concatenate(names[h * NX : (h + 1) * NX], axis=1),
                jnp.zeros((6, NX * TOK), F32),
            ],
            axis=0,
        )
        rows = lax.dot_general(
            values.astype(BF16), sel[h], (((1,), (1,)), ((), ())), preferred_element_type=F32
        )
        rowblk[h] = jnp.concatenate([rows, jnp.zeros((8, 256 - CH), F32)], axis=1)
    for pair in z_starts(1, rowblk, m_rows):
        z_go(pair)
    rowmeta[0] = rowblk[mine]

    lane_iota = lax.broadcasted_iota(jnp.int32, (CAP, CH), 1)

    def compact(g):
        total = jnp.zeros((CAP, CH), F32)
        for b in range(NX):
            inside = (lane_iota >= b * CAP) & (lane_iota < (b + 1) * CAP)
            total = total + jnp.where(inside, g[b * CAP : (b + 1) * CAP], 0.0)
        return total

    def gram(block):
        return compact(
            lax.dot_general(block, block, (((1,), (1,)), ((), ())), preferred_element_type=F32)
        )

    def widen(g):
        return jnp.concatenate([g, jnp.zeros((CAP, 256 - CH), F32)], axis=1)

    eye = (
        lax.broadcasted_iota(jnp.int32, (CH, CH), 0) == lax.broadcasted_iota(jnp.int32, (CH, CH), 1)
    ).astype(BF16)

    def remote(src, dst, ssem, rsem, dev):
        return pltpu.make_async_remote_copy(
            src_ref=src, dst_ref=dst, send_sem=ssem, recv_sem=rsem, device_id=dev, device_id_type=MESH
        )

    def source_products():
        for h in range(2):
            gcs[h] = widen(gram(cblk[h]))
        z_go((tp != z, lambda: remote(gcs, gcr.at[tp], gs_s.at[0], gs_r.at[tp], (ep, z))))

    def owner_products():
        @pl.when(tp == z)
        def _():
            gcr[z] = gcs[...]
            for d in range(1, TP):
                arrived(gcr.at[(tp + d) % TP], gs_s.at[0], gs_r.at[(tp + d) % TP])
            for h in range(2):
                rows = rowblk[h][:, :CH]
                cols = lax.dot_general(
                    eye, rows.astype(BF16), (((1,), (1,)), ((), ())), preferred_element_type=F32
                )
                weight = jnp.where(cols[:, 1:2] == rows[1:2], cols[:, 0:1] * rows[0:1], 0.0)
                total = gcr[0, h]
                for j in range(1, TP):
                    total = total + gcr[j, h]
                wcs[h] = widen(compact(weight)) * total
            wc[z] = wcs[mine]

        for d in range(1, NZ):
            zd = (z + d) % NZ
            z_go((
                tp == z,
                lambda zd=zd, d=d: remote(wcs.at[zd // 4], wc.at[z], wz_s.at[d], wz_r.at[0], (x * NZ + zd, tp)),
            ))

    def gather_products():
        @pl.when(tp != z)
        def _():
            arrived(wc.at[tp], wz_s.at[1], wz_r.at[0])

        for i in (1, 2, 3):
            send(wc.at[tp], wc.at[tp], wc_s.at[i], wc_r.at[i], (ep, ((y + i) % 4) * 2 + core))
        send(wc.at[tp], wc.at[tp], wb_s.at[0], wb_r.at[0], (ep, sib))

    def take_c(k):
        if k > 0:
            arrived(cf.at[rows_of(k)], zs_s.at[2, k], zs_r.at[2, k])
            z_go(z_forward(2, c_rows, k))
            arrived(rowmeta.at[k], zs_s.at[1, k], zs_r.at[1, k])
            z_go(z_forward(1, m_rows, k))
        rows = rowmeta[k][:, :CH]
        cols = lax.dot_general(eye, rows.astype(BF16), (((1,), (1,)), ((), ())), preferred_element_type=F32)
        colg[rows_of(k)] = cols[:, 0:1]
        cold[rows_of(k)] = cols[:, 1:2]


    def build_c():
        x_wait(2, craw)
        raw = craw[...].reshape(NX * 2 * CAP, SH)
        for h in range(2):
            cblk[h] = jnp.dot(perm[h], raw, preferred_element_type=F32).astype(BF16)
        cf[rows_of(0)] = cblk[mine]

    def hidden_spread(p):
        spread(hf, pl.ds(p * PAIR, PAIR), p, hy_s, hy_r, hb_s, hb_r)

    def hidden_pass(p):
        pass_on(hf, pl.ds(p * PAIR, PAIR), p, hy_s, hy_r, h2_s, h2_r, hb_s, hb_r)

    def hidden_last(p):
        last_hop(hf, pl.ds(p * PAIR, PAIR), p, h2_s, h2_r, hb_s, hb_r)

    def hidden_chunk(k):
        rows = rows_of(k)
        accg[...] = jnp.zeros_like(accg)
        accu[...] = jnp.zeros_like(accu)

        @pl.loop(0, TP)
        def _(j):
            depth = pl.ds(pl.multiple_of(j * SH, SH), SH)
            block = xf[j, rows, :]
            accg[...] += jnp.dot(block, wg[0, depth, :], preferred_element_type=F32)
            accu[...] += jnp.dot(block, wu[0, depth, :], preferred_element_type=F32)

        g = accg[...]
        h = (g / (1.0 + jnp.exp(-g)) * accu[...]).astype(BF16)
        hf[tp, rows, :] = h
        if k == 5 or k == 7:
            hidden_spread(k // 2)
        hg[k] = gram(h)

    def shares():
        terms, named = [], []
        base = jnp.zeros((NZ, 128), jnp.int32)
        chunk_iota = lax.broadcasted_iota(jnp.int32, (NZ, 128), 0)
        for k in range(NZ):
            terms.append(jnp.sum(wc[source_at[k]][:, :CH] * hg[k], axis=0, keepdims=True))
            named.append(rowmeta[k][1:2, :CH])
            base = jnp.where(chunk_iota == k, source_at[k] * 4, base)
        term = jnp.concatenate(terms, axis=0)
        name = jnp.concatenate(named, axis=0)
        first = base[:, 0:1].astype(F32)
        lanes = lax.broadcasted_iota(jnp.int32, (NZ, 128), 1)
        total = jnp.zeros((NZ, 128), F32)
        for xs_ in range(NX):
            for ex in range(4):
                number = xs_ * 4 * NZ + ex
                one = jnp.sum(jnp.where(name == first + float(number), term, 0.0), axis=1, keepdims=True)
                total = total + jnp.where(lanes == base + number, one, 0.0)
        return jnp.broadcast_to(jnp.sum(total, axis=0, keepdims=True), (8, 128))

    x_events = {0: (1,), 1: (2,), 2: (3,), 3: (4,), 4: (5,), 5: (6,), 6: (7,)}
    c_events = {3: (0, 1), 4: (2,), 5: (3,), 6: (4,), 7: (5,), 8: (6,), 9: (7,)}
    for s in range(NZ + 3):
        if s == 0:
            spread(xf, rows_of(0), 0, ys_s, ys_r, sb_s, sb_r)
        for k in x_events.get(s, ()):
            arrived(xf.at[tp, rows_of(k)], zs_s.at[0, k], zs_r.at[0, k])
            z_go(z_forward(0, x_rows, k))
            spread(xf, rows_of(k), k, ys_s, ys_r, sb_s, sb_r)
        k = s - 1
        if 0 <= k < NZ:
            pass_on(xf, rows_of(k), k, ys_s, ys_r, y2_s, y2_r, sb_s, sb_r)
        if s == 0:
            build_c()
            source_products()
        if s == 1:
            for pair in z_starts(2, cblk, c_rows):
                z_go(pair)
        k = s - 2
        if 0 <= k < NZ:
            last_hop(xf, rows_of(k), k, y2_s, y2_r, sb_s, sb_r)
        if s == NZ:
            for p in range(2):
                hidden_spread(p)
        for k in c_events.get(s, ()):
            take_c(k)
        if s == 3:
            owner_products()
        if s == 5:
            gather_products()
        if s == 7:
            for i in (1, 2, 3):
                j = ((y + i) % 4) * 2 + core
                arrived(wc.at[j], wc_s.at[i], wc_r.at[4 - i])
                send(wc.at[j], wc.at[j], wb_s.at[i], wb_r.at[4 - i], (ep, sib))
        if s == 10:
            hidden_pass(0)
        k = s - 3
        if 0 <= k < NZ:
            if k == 0:
                for c in wcopies:
                    c.wait()
            from_sibling(xf, rows_of(k), k, sb_s, sb_r)
            hidden_chunk(k)

    for i in range(4):
        arrived(wc.at[((y + i) % 4) * 2 + 1 - core], wb_s.at[i], wb_r.at[(4 - i) % 4])
    partial = shares()

    def exchange_start(value, buf, count, me, device_of, ssem, rsem):
        buf[me] = value
        for d in range(1, count):
            send(buf.at[me], buf.at[me], ssem.at[d], rsem.at[d], device_of((me + d) % count))

    def exchange_end(buf, count, me, ssem, rsem):
        for d in range(1, count):
            arrived(buf.at[(me + count - d) % count], ssem.at[d], rsem.at[d])
        total = buf[0]
        for j in range(1, count):
            total = total + buf[j]
        return total

    exchange_start(partial, nz, NZ, z, lambda j: (x * NZ + j, tp), nz_s, nz_r)
    hidden_pass(1)
    total = exchange_end(nz, NZ, z, nz_s, nz_r)
    exchange_start(total, nx, NX, x, lambda j: (j * NZ + z, tp), nx_s, nx_r)
    hidden_last(0)
    hidden_pass(2)
    total = exchange_end(nx, NX, x, nx_s, nx_r)
    exchange_start(total, nt, TP, tp, lambda j: (ep, j), nt_s, nt_r)
    hidden_last(1)
    hidden_pass(3)
    hidden_last(2)
    total = exchange_end(nt, TP, tp, nt_s, nt_r)

    clip_level = CLIP_SCALE * (FF * D) ** 0.5
    norm = jnp.sqrt(total[0:1])
    ratio[...] = norm / clip_level
    factor = clip_level / jnp.maximum(norm, clip_level)

    name_iota = lax.broadcasted_iota(jnp.int32, (CH, 128), 1).astype(F32)
    for k in range(NZ):
        hit = jnp.where(name_iota == cold[rows_of(k)], factor, 0.0)
        slot_factor = jnp.sum(hit, axis=1, keepdims=True)
        scale = slot_factor * colg[rows_of(k)]
        cs_k = (scale * cf[rows_of(k)].astype(F32)).astype(BF16)
        outs[rows_of(k)] = cs_k

    hidden_last(3)
    for p in range(4):
        from_sibling(hf, pl.ds(p * PAIR, PAIR), p, hb_s, hb_r)

    @pl.loop(0, TP)
    def _(j):
        block = lax.dot_general(
            hf[j], outs[...], (((0,), (0,)), ((), ())), preferred_element_type=F32
        )
        piece = pl.ds(pl.multiple_of(j * UN, UN), UN)
        outv[piece, :] = block.astype(BF16)
        pltpu.make_async_copy(outv.at[piece], out_hbm.at[0, piece], osem.at[j]).start()

    for pair in zsent:
        sent_if(pair)
    for c in sends:
        c.wait_send()

    @pl.loop(0, TP)
    def _(j):
        piece = pl.ds(pl.multiple_of(j * UN, UN), UN)
        pltpu.make_async_copy(outv.at[piece], out_hbm.at[0, piece], osem.at[j]).wait()


def body(tokens, cotangent, routes, route_gates, example_ids, gate_weight, up_weight):
    anywhere = pl.BlockSpec(memory_space=pl.ANY)
    dma = pltpu.SemaphoreType.DMA
    vm = pltpu.VMEM
    inside = pl.BlockSpec(memory_space=vm)
    update, ratio = pl.pallas_call(
        kernel,
        out_shape=(
            jax.ShapeDtypeStruct((1, TP * UN, SH), BF16),
            jax.ShapeDtypeStruct((1, 128), F32),
        ),
        in_specs=[anywhere, anywhere, inside, inside, inside, anywhere, anywhere],
        out_specs=(anywhere, inside),
        scratch_shapes=[
            vm((TOK, SH), BF16),
            vm((TOK, SH), BF16),
            vm((NX, 8, TOK), F32),
            vm((NX, 2 * CAP, SH), BF16),
            vm((NX, 2 * CAP, SH), BF16),
            vm((NX, 2 * CAP, SH), BF16),
            vm((NX, 2 * CAP, SH), BF16),
            vm((2, CH, NX * TOK), BF16),
            vm((2, CH, NX * 2 * CAP), BF16),
            vm((2, CH, SH), BF16),
            vm((2, CH, SH), BF16),
            vm((2, 8, 256), F32),
            vm((NZ, 8, 256), F32),
            vm((TP, SLOTS, SH), BF16),
            vm((SLOTS, SH), BF16),
            vm((SLOTS, SH), BF16),
            vm((TP, SLOTS, UN), BF16),
            vm((1, D, UN), BF16),
            vm((1, D, UN), BF16),
            vm((CH, UN), F32),
            vm((CH, UN), F32),
            vm((TP * UN, SH), BF16),
            vm((2, CAP, 256), F32),
            vm((TP, 2, CAP, 256), F32),
            vm((2, CAP, 256), F32),
            vm((NZ, CAP, CH), F32),
            vm((TP, CAP, 256), F32),
            vm((SLOTS, 1), F32),
            vm((SLOTS, 1), F32),
            vm((NZ, 8, 128), F32),
            vm((NX, 8, 128), F32),
            vm((TP, 8, 128), F32),
            dma((2,)),
            dma((4,)),
            dma((TP,)),
            dma((3, NX)), dma((3, NX)),
            dma((3, NZ + 2)), dma((3, NZ)),
            dma((2, NZ)), dma((2, NZ)),
            dma((NZ,)), dma((NZ,)),
            dma((4, NZ)), dma((4, NZ)),
            dma((2, 4)), dma((2, 4)),
            dma((4,)), dma((4,)),
            dma((4, 4)), dma((4, 4)),
            dma((1,)), dma((TP,)),
            dma((NZ,)), dma((1,)),
            dma((4,)), dma((4,)),
            dma((4,)), dma((4,)),
            dma((NZ,)), dma((NZ,)),
            dma((NX,)), dma((NX,)),
            dma((TP,)), dma((TP,)),
        ],
        compiler_params=pltpu.CompilerParams(
            collective_id=0, has_side_effects=True, vmem_limit_bytes=58 * 1024 * 1024
        ),
        cost_estimate=pl.CostEstimate(
            flops=12_000_000_000, bytes_accessed=10_000_000, transcendentals=327_680
        ),
        name="moe_clip",
    )(tokens, cotangent, routes.T, route_gates.T, example_ids, gate_weight, up_weight)
    return (update, ratio.reshape(128))


def solution(mesh):
    placed = (
        P("ep", "tp"),
        P("ep", "tp"),
        P("ep", None),
        P("ep", None),
        P("ep", None),
        P("ep", None, "tp"),
        P("ep", None, "tp"),
    )
    return jax.shard_map(
        body, mesh=mesh, in_specs=placed, out_specs=(P("ep", None, "tp"), P()), check_vma=False
    )
```
